128 devices in a mesh: cam: 4 (over x), tile: 32 (over y, z, core).
Axes of the slice: x: 4, y: 4, z: 4, core: 2. Of those that a mesh axis runs over, the one named last changes fastest.
Arguments:
- patches: bfloat16 [4, 4096, 1024], P('cam', 'tile'), may hold values from -6 to 6
- vit_gain: float32 [1024], replicated, may hold values from 0.25 to 1.75
- vit_qkv: bfloat16 [1024, 3072], replicated, may hold values from -3.75 to 3.75
- vit_qkv_bias: float32 [3072], replicated, may hold values from -3 to 3
- vit_proj: bfloat16 [1024, 1024], replicated, may hold values from -0.1875 to 0.1875
- vit_scale: float32 [1024], replicated, may hold values from 0.5 to 2.5
- point_feats: bfloat16 [262144, 512], P(('cam', 'tile')), may hold values from -6 to 6
- point_order: int32 [128, 2048], P(('cam', 'tile')), may hold values from 0 to 2047, each once within a row
- window_ids: int32 [128, 2048], P(('cam', 'tile')), may hold values from 0 to 3, never falling along the last dimension, each value on 1 to 1024 neighbouring positions
- point_tile: int32 [262144, 1], P(('cam', 'tile')), may hold values from 0 to 127; in each aligned block of 2048 rows (0 to 2047, 2048 to 4095, ...) at most 24 rows name the same one
- point_patch: int32 [262144], P(('cam', 'tile')), may hold values from 0 to 127
- pt_gain: float32 [2, 512], replicated, may hold values from 0.25 to 1.75
- pt_qkv: bfloat16 [512, 768], replicated, may hold values from -13.258252 to 13.258252
- pt_proj: bfloat16 [256, 512], replicated, may hold values from -0.375 to 0.375
- pt_up: bfloat16 [512, 2048], replicated, may hold values from -0.25 to 0.25
- pt_down: bfloat16 [2048, 512], replicated, may hold values from -0.125 to 0.125
- head_w: bfloat16 [512, 1024], replicated, may hold values from -0.25 to 0.25
Outputs:
- point_out: bfloat16 [262144, 512], P(('cam', 'tile'))
- cos_loss: float32 [262144], P(('cam', 'tile'))
The draws below stay inside these ranges and needn't reach their ends.
Inputs may be any that keep to these rules, and one draw needn't show every extreme that they name: `point_order`: each row is a permutation of 0 to 2047. `window_ids`: never falling along a row; each window holds 1 to 1024 positions and some window exactly 1024. `point_tile`: among the points of one block no tile is named more than 24 times, a bound that some block reaches.
All inputs are finite; a program needn't handle non-finite values.
Results may differ from the reference program's by a relative error of at most 0.0045.
The reference program's roundings to bfloat16 on the way count: a program that leaves them out, or rounds other values in their place, can miss the bound.
Values may be sent and summed in bfloat16 or wider, within the bound.
No kernel may reach another device: no remote copies, remote signals or barrier semaphores. Data moves between devices by JAX's collectives and lax.ppermute only.
A program may use at most 256 MiB of HBM per device.

```python
import math
import jax
import jax.numpy as jnp
import numpy as np
from jax import lax

DV = 1024
HD_V = 64
HEADS_V = 16
C = 512
HEADS_P = 16
HD_P = 16
ATT = 256
MLP = 2048
TILE = 128
WIN = 1024
PT_DEV = 2048
GROUP = 4096
POINTS = 262144
CAP = 24
NWIN = 4
N_CAM = 4
N_TILE = 32


def draw_patches(key, part):
    key = jax.random.fold_in(key, 11)
    values = jax.random.normal(key, (N_CAM * GROUP, DV), jnp.float32)
    return jnp.clip(values, -6.0, 6.0).reshape(N_CAM, GROUP, DV).astype(jnp.bfloat16)


def draw_point_feats(key, part):
    key = jax.random.fold_in(key, 12)
    values = jax.random.normal(key, (POINTS, C), jnp.float32)
    return jnp.clip(values, -6.0, 6.0).astype(jnp.bfloat16)


def draw_vit_qkv(key, part):
    key = jax.random.fold_in(key, 13)
    return (jnp.clip(jax.random.normal(key, (DV, 3 * DV), jnp.float32), -6.0, 6.0) * DV ** (-0.5)).astype(jnp.bfloat16)


def draw_pt_qkv(key, part):
    key = jax.random.fold_in(key, 14)
    return (jnp.clip(jax.random.normal(key, (C, 3 * ATT), jnp.float32), -6.0, 6.0) * C ** (-0.5)).astype(jnp.bfloat16)


def with_ends(entries, rng, smallest, largest):
    longest = entries.shape.index(max(entries.shape))
    spots = []
    for shift in (0, 1):
        where = [jax.random.randint(jax.random.fold_in(rng, axis), (), 0, length) for axis, length in enumerate(entries.shape)]
        where[longest] = (where[longest] + shift) % entries.shape[longest]
        spots.append(tuple(where))
    return entries.at[spots[0]].set(smallest).at[spots[1]].set(largest)


def length_profile(amount, total, bound, slope):
    weights = [(1 << 20) // math.isqrt(rank ** slope) + 1 for rank in range(2, amount + 1)]
    surplus, holding = total - bound - (amount - 1), [1] * (amount - 1)
    while surplus > 0:
        candidates = [i for i in range(amount - 1) if holding[i] < bound]
        whole, budget = sum([weights[i] for i in candidates]), surplus
        for i in candidates:
            addition = min(bound - holding[i], max(1, budget * weights[i] // whole), surplus)
            holding[i] = holding[i] + addition
            surplus = surplus - addition
    return np.array([bound] + holding)


def uneven_parts(stream_key, count, total, reach, skew):
    if count == 2:
        one = jax.random.randint(stream_key, (), max(1, total - reach), min(reach, total - 1) + 1)
        return jnp.stack([one, total - one])
    sizes = jnp.asarray(length_profile(count, total, reach, skew), jnp.int32)
    twos = (count - 1) // 2
    source_of, receiver = sizes[1:1 + 2 * twos:2], sizes[2:2 + 2 * twos:2]
    slack = jnp.minimum(source_of - 1, reach - receiver)
    shifted = jax.random.randint(jax.random.fold_in(stream_key, 1), (twos,), 0, 1 << 20) % (slack + 1)
    sizes = sizes.at[1:1 + 2 * twos:2].set(source_of - shifted).at[2:2 + 2 * twos:2].set(receiver + shifted)
    return sizes[jax.random.permutation(jax.random.fold_in(stream_key, 2), count)]


def assign_block(rng, own, number, rows, count, top, most, skew):
    sequence = jax.random.permutation(rng, count)
    packed, common = portions_of(count, rows * top, most, skew, True), portions_of(count, rows * top, most, skew, False)
    places = jnp.arange(count)

    def named(lengths, turn):
        used = int((lengths > 0).sum())
        fixed = max(1, used // 4)
        passed = fixed + (places - fixed + turn * (used - fixed)) % max(1, count - fixed)
        return jnp.zeros((count,), jnp.int32).at[sequence[jnp.where(places < fixed, places, passed)]].set(jnp.asarray(lengths, jnp.int32))

    lengths = jnp.where(number % 4 == 0, named(packed, number // 4), named(common, number - number // 4 - 1))
    mixed = jax.random.permutation(jax.random.fold_in(own, 3), count)
    giver, sink = mixed[0:count // 2 * 2:2], mixed[1:count // 2 * 2:2]
    room = jnp.minimum(lengths[giver] - 1, most - lengths[sink]) // 2
    room = jnp.where((giver == sequence[0]) | (sink == sequence[0]) | (lengths[sink] == 0), 0, jnp.maximum(room, 0))
    passed = jax.random.randint(jax.random.fold_in(own, 4), (count // 2,), 0, 1 << 20) % (room + 1)
    lengths = lengths.at[giver].add(-passed).at[sink].add(passed)
    members = jnp.searchsorted(jnp.cumsum(lengths), jnp.arange(rows * top), side="right").astype(jnp.int32)
    grid = members.reshape(top, rows).T
    grid = grid[jax.random.permutation(jax.random.fold_in(own, 1), rows)]
    turn = jax.random.randint(jax.random.fold_in(own, 2), (rows, 1), 0, top)
    return jnp.take_along_axis(grid, (jnp.arange(top)[None, :] + turn) % top, axis=1)


def portions_of(count, total, most, slope, full):
    weights = [(1 << 20) // math.isqrt(grade ** slope) + 1 for grade in range(1, count + 1)]
    largest = most if full else min(most, max(-(-total // count), total * weights[0] // sum(weights)))
    least = 1 if total - largest >= count - 1 else 0
    holding, rest = [largest] + [least] * (count - 1), total - largest - least * (count - 1)
    while rest > 0:
        movable = [i for i in range(1, count) if holding[i] < largest] or [i for i in range(1, count) if holding[i] < most]
        pool, remaining = sum([weights[i] for i in movable]), rest
        for i in movable:
            more = min(most - holding[i], max(1, remaining * weights[i] // pool), rest)
            holding[i] = holding[i] + more
            rest = rest - more
    return np.array(holding)


def centred(rng, extent, scale, reach, held_as=jnp.bfloat16):
    return jnp.clip(scale * jax.random.normal(rng, extent, jnp.float32), -reach, reach).astype(held_as)


def setup_inputs(seed: int = 0) -> dict:
    key_of = jax.random.split(jax.random.key(seed), 18)
    patches = draw_patches(jax.random.fold_in(key_of[17], 71), 0)
    vit_gain = jnp.clip(1.0 + 0.15 * jax.random.normal(key_of[1], (DV,), jnp.float32), 0.25, 1.75)
    vit_qkv = draw_vit_qkv(jax.random.fold_in(key_of[17], 71), 0)
    vit_qkv_bias = centred(key_of[3], (3 * DV,), 0.5, 3.0, jnp.float32)
    vit_proj = centred(key_of[4], (DV, DV), DV ** -0.5, 0.1875)
    vit_scale = jnp.clip(jnp.exp(jax.random.uniform(key_of[5], (DV,), jnp.float32, math.log(0.5), math.log(2.5))), 0.5, 2.5)
    point_feats = draw_point_feats(jax.random.fold_in(key_of[17], 71), 0)
    point_order = jax.vmap(lambda own: jax.random.permutation(own, PT_DEV))(jax.random.split(key_of[7], (N_CAM * N_TILE))).reshape((N_CAM * N_TILE, PT_DEV)).astype(jnp.int32)
    window_ids = jax.vmap(lambda own: jnp.searchsorted(jnp.cumsum(uneven_parts(own, NWIN, PT_DEV, WIN, 2)), jnp.arange(PT_DEV), side="right"))(jax.random.split(key_of[8], (N_CAM * N_TILE))).reshape((N_CAM * N_TILE, PT_DEV)).astype(jnp.int32)
    point_tile_keys = jax.random.split(jax.random.fold_in(key_of[9], 1), POINTS // PT_DEV)
    point_tile_turns = jax.random.permutation(jax.random.fold_in(key_of[9], 3), POINTS // PT_DEV)
    point_tile = jax.vmap(lambda own, number: assign_block(jax.random.fold_in(key_of[9], 2), own, number, PT_DEV, N_CAM * N_TILE, 1, CAP, 2))(point_tile_keys, point_tile_turns).reshape((POINTS, 1))
    point_patch = with_ends(jax.random.randint(key_of[10], (POINTS,), 0, TILE), jax.random.fold_in(key_of[10], 1), 0, TILE - 1).astype(jnp.int32)
    pt_gain = jnp.clip(1.0 + 0.15 * jax.random.normal(key_of[11], (2, C), jnp.float32), 0.25, 1.75)
    pt_qkv = draw_pt_qkv(jax.random.fold_in(key_of[17], 71), 0)
    pt_proj = centred(key_of[13], (ATT, C), ATT ** -0.5, 0.375)
    pt_up = centred(key_of[14], (C, MLP), C ** -0.5, 0.25)
    pt_down = centred(key_of[15], (MLP, C), MLP ** -0.5, 0.125)
    head_w = centred(key_of[16], (C, DV), C ** -0.5, 0.25)
    return {"patches": patches, "vit_gain": vit_gain, "vit_qkv": vit_qkv, "vit_qkv_bias": vit_qkv_bias, "vit_proj": vit_proj, "vit_scale": vit_scale, "point_feats": point_feats, "point_order": point_order, "window_ids": window_ids, "point_tile": point_tile, "point_patch": point_patch, "pt_gain": pt_gain, "pt_qkv": pt_qkv, "pt_proj": pt_proj, "pt_up": pt_up, "pt_down": pt_down, "head_w": head_w}


eps_norm = 1e-06

def layer_norm(values, gain):
    center = values - lax.optimization_barrier(jnp.mean(values, -1, keepdims=True))
    spread = lax.optimization_barrier(jnp.mean(center * center, -1, keepdims=True))
    return center * lax.rsqrt(spread + eps_norm) * gain

def vit_group(group_rows, vit_gain, vit_qkv, vit_qkv_bias, vit_proj, vit_scale):
    inputs = group_rows.astype(jnp.float32)
    normed = layer_norm(inputs, vit_gain).astype(jnp.bfloat16)
    mixture = (jnp.dot(normed, vit_qkv, preferred_element_type=jnp.float32) + vit_qkv_bias).astype(jnp.bfloat16)

    def split_heads(block_cols):
        return block_cols.reshape(GROUP, HEADS_V, HD_V).transpose(1, 0, 2)
    query_heads = split_heads(mixture[:, :DV])
    key_heads = split_heads(mixture[:, DV:2 * DV])
    value_heads = split_heads(mixture[:, 2 * DV:])

    def one_head(head_inputs):
        query_rows, key_rows, value_rows = head_inputs
        scores = jnp.dot(query_rows, key_rows.T, preferred_element_type=jnp.float32) * HD_V ** (-0.5)
        row_max = lax.optimization_barrier(jnp.max(scores, -1, keepdims=True))
        exps = jnp.exp(scores - row_max)
        sums = lax.optimization_barrier(jnp.sum(exps, -1, keepdims=True))
        return jnp.dot(exps.astype(jnp.bfloat16), value_rows, preferred_element_type=jnp.float32) / sums
    attended = lax.map(one_head, (query_heads, key_heads, value_heads))
    attended = attended.transpose(1, 0, 2).reshape(GROUP, DV).astype(jnp.bfloat16)
    return (inputs + vit_scale * jnp.dot(attended, vit_proj, preferred_element_type=jnp.float32)).astype(jnp.bfloat16)

def window_attention(query_rows, key_rows, value_rows, windows):
    point_count = query_rows.shape[0]
    query_heads = query_rows.reshape(point_count, HEADS_P, HD_P).transpose(1, 0, 2).astype(jnp.float32)
    key_heads = key_rows.reshape(point_count, HEADS_P, HD_P).transpose(1, 0, 2).astype(jnp.float32)
    value_heads = value_rows.reshape(point_count, HEADS_P, HD_P).transpose(1, 0, 2).astype(jnp.float32)
    scores = jnp.einsum('hqd,hkd->hqk', query_heads, key_heads) * HD_P ** (-0.5)
    same_window = (windows[:, None] == windows[None, :])[None]
    scores = jnp.where(same_window, scores, -1e+30)
    row_max = lax.optimization_barrier(jnp.max(scores, -1, keepdims=True))
    exps = jnp.exp(scores - row_max)
    sums = lax.optimization_barrier(jnp.sum(exps, -1, keepdims=True))
    weights = exps.astype(jnp.bfloat16).astype(jnp.float32)
    attended = jnp.einsum('hqk,hkd->hqd', weights, value_heads) / sums
    return attended.transpose(1, 0, 2).reshape(point_count, ATT).astype(jnp.bfloat16)

def reference(patches, vit_gain, vit_qkv, vit_qkv_bias, vit_proj, vit_scale, point_feats, point_order, window_ids, point_tile, point_patch, pt_gain, pt_qkv, pt_proj, pt_up, pt_down, head_w):

    def teacher_group(group_rows):
        return vit_group(group_rows, vit_gain, vit_qkv, vit_qkv_bias, vit_proj, vit_scale)
    teacher = lax.map(teacher_group, patches)
    teacher_flat = teacher.reshape(N_CAM * GROUP, DV)
    block_count = N_CAM * N_TILE
    feats_blocks = point_feats.reshape(block_count, PT_DEV, C)
    tile_blocks = point_tile.reshape(block_count, PT_DEV)
    patch_blocks = point_patch.reshape(block_count, PT_DEV)

    def one_block(block_inputs):
        feats, ordering, windows, tile_ids, patch_ids = block_inputs
        serial = jnp.take(feats, ordering.astype(jnp.int32), axis=0).astype(jnp.float32)
        normed = layer_norm(serial, pt_gain[0]).astype(jnp.bfloat16)
        mixture = jnp.dot(normed, pt_qkv, preferred_element_type=jnp.float32).astype(jnp.bfloat16)
        attended = window_attention(mixture[:, :ATT], mixture[:, ATT:2 * ATT], mixture[:, 2 * ATT:], windows)
        residual = serial + jnp.dot(attended, pt_proj, preferred_element_type=jnp.float32)
        normed_two = layer_norm(residual, pt_gain[1]).astype(jnp.bfloat16)
        hidden = jax.nn.gelu(jnp.dot(normed_two, pt_up, preferred_element_type=jnp.float32), approximate=False).astype(jnp.bfloat16)
        block_out = (residual + jnp.dot(hidden, pt_down, preferred_element_type=jnp.float32)).astype(jnp.bfloat16)
        student = jnp.dot(block_out, head_w, preferred_element_type=jnp.float32)
        row_ids = (tile_ids * TILE + patch_ids).astype(jnp.int32)
        target = jnp.take(teacher_flat, row_ids, axis=0).astype(jnp.float32)
        inner = lax.optimization_barrier(jnp.sum(student * target, -1))
        norms = jnp.sqrt(lax.optimization_barrier(jnp.sum(student * student, -1)) + eps_norm) * jnp.sqrt(lax.optimization_barrier(jnp.sum(target * target, -1)) + eps_norm)
        return (block_out, 1.0 - inner / norms)
    outs, losses = lax.map(one_block, (feats_blocks, point_order, window_ids, tile_blocks, patch_blocks))
    return (outs.reshape(POINTS, C), losses.reshape(POINTS))
```

```python
import functools

import jax
import jax.numpy as jnp
from jax import lax
from jax.experimental import pallas as pl
from jax.experimental.pallas import tpu as pltpu
from jax.sharding import PartitionSpec as P

HD_V = 64
HD_P = 16
CAP = 24
eps_norm = 1e-06
BIG = 1e30
MIB = 1024 * 1024
F32 = jnp.float32
BF16 = jnp.bfloat16
NT = (((1,), (1,)), ((), ()))
TN = (((0,), (0,)), ((), ()))
MIX_STEP = 512
BLOCK_STEP = 512
HIDDEN = 512
LOSS_STEP = 512


def layer_norm(values, gain):
    center = values - jnp.mean(values, -1, keepdims=True)
    spread = jnp.mean(center * center, -1, keepdims=True)
    return center * lax.rsqrt(spread + eps_norm) * gain


def dot(left, right, dims=None):
    if dims is None:
        return jnp.dot(left, right, preferred_element_type=F32)
    return lax.dot_general(left, right, dims, preferred_element_type=F32)


def lanes(shape):
    return lax.broadcasted_iota(jnp.int32, shape, len(shape) - 1)


def whole(shape):
    return pl.BlockSpec(shape, lambda *_: (0,) * len(shape))


def params(limit=48):
    return pltpu.CompilerParams(vmem_limit_bytes=limit * MIB)


def cost(macs, moved, exps=0):
    return pl.CostEstimate(flops=2 * macs, bytes_accessed=moved, transcendentals=exps)


def teacher_mix_kernel(x_ref, gain_ref, wq_ref, wk_ref, wv_ref, bq_ref, bk_ref, bv_ref, out_ref, normed):
    @pl.when(pl.program_id(0) == 0)
    def _():
        normed[...] = layer_norm(x_ref[...].astype(F32), gain_ref[...]).astype(BF16)

    rows = normed[...]
    for part, (w_ref, b_ref) in enumerate(((wq_ref, bq_ref), (wk_ref, bk_ref), (wv_ref, bv_ref))):
        mixed = (dot(rows, w_ref[...]) + b_ref[...]).astype(BF16).astype(F32)
        if part == 0:
            mixed = mixed * HD_V ** (-0.5)
        turned = mixed.T.astype(BF16)
        for head in range(turned.shape[0] // HD_V):
            piece = turned[head * HD_V : (head + 1) * HD_V]
            for core in range(2):
                out_ref[2 * head + core, part * HD_V : (part + 1) * HD_V, :] = piece


def teacher_mix(patches, gain, weights, bias):
    rows, width = patches.shape
    heads = width // HD_V
    step = 256
    steps = width // step

    def col(part):
        return pl.BlockSpec((width, step), lambda i: (0, part * steps + i))

    def bias_col(part):
        return pl.BlockSpec((1, step), lambda i: (0, part * steps + i))

    return pl.pallas_call(
        teacher_mix_kernel,
        grid=(steps,),
        in_specs=[whole((rows, width)), whole((1, width))]
        + [col(p) for p in range(3)]
        + [bias_col(p) for p in range(3)],
        out_specs=pl.BlockSpec((2 * step // HD_V, 3 * HD_V, rows), lambda i: (i, 0, 0)),
        out_shape=jax.ShapeDtypeStruct((2 * heads, 3 * HD_V, rows), BF16),
        scratch_shapes=[pltpu.VMEM((rows, width), BF16)],
        compiler_params=params(),
        cost_estimate=cost(rows * width * 3 * width, 8 * MIB),
        name="teacher_mix",
    )(patches, gain, weights, weights, weights, bias, bias, bias)


def teacher_attention_kernel(core_ref, mix_ref, out_ref, keys, values, scores):
    tiles, _, rows = mix_ref.shape
    step = pl.program_id(0)

    @pl.when(step == 0)
    def _():
        for tile in range(tiles):
            span = slice(tile * rows, (tile + 1) * rows)
            keys[:, span] = mix_ref[tile, HD_V : 2 * HD_V, :]
            turned = mix_ref[tile, 2 * HD_V :, :].astype(F32)
            values[span, :] = jnp.concatenate([turned, jnp.ones_like(turned)], 0).T.astype(BF16)

    core = core_ref[0]
    first = mix_ref[4 * step + core, :HD_V, :].astype(F32)
    second = mix_ref[4 * step + 2 + core, :HD_V, :].astype(F32)
    queries = jnp.concatenate([first, second], 1).T.astype(BF16)
    count = tiles * rows
    chunk = 1024
    top = None
    for start in range(0, count, chunk):
        part = dot(queries, keys[:, start : start + chunk])
        scores[:, start : start + chunk] = part
        for lane in range(0, chunk, 128):
            piece = part[:, lane : lane + 128]
            top = piece if top is None else jnp.maximum(top, piece)
    top = jnp.max(top, -1, keepdims=True)
    total = None
    for start in range(0, count, chunk):
        exps = jnp.exp(scores[:, start : start + chunk] - top).astype(BF16)
        part = dot(exps, values[start : start + chunk, :])
        total = part if total is None else total + part
    turned = total.T
    attended = (turned[:HD_V] / turned[HD_V:]).astype(BF16)
    out_ref[0] = attended[:, :rows]
    out_ref[1] = attended[:, rows:]


def teacher_attention(core, mix):
    tiles, depth, rows = mix.shape
    return pl.pallas_call(
        teacher_attention_kernel,
        grid_spec=pltpu.PrefetchScalarGridSpec(
            num_scalar_prefetch=1,
            grid=(tiles // 4,),
            in_specs=[whole((tiles, depth, rows))],
            out_specs=pl.BlockSpec((2, HD_V, rows), lambda i, c: (i, 0, 0)),
            scratch_shapes=[
                pltpu.VMEM((HD_V, tiles * rows), BF16),
                pltpu.VMEM((tiles * rows, 128), BF16),
                pltpu.VMEM((2 * rows, tiles * rows), F32),
            ],
        ),
        out_shape=jax.ShapeDtypeStruct((tiles // 2, HD_V, rows), BF16),
        compiler_params=params(),
        cost_estimate=cost(2 * tiles * rows * tiles * rows * 128, 2 * MIB, tiles * rows * tiles * rows // 2),
        name="teacher_attention",
    )(core, mix)


def teacher_reply_kernel(me_ref, att_ref, patches_ref, proj_ref, scale_ref, head_ref, asked_ref, out_ref, seen):
    @pl.when(pl.program_id(0) == 0)
    def _():
        heads, depth, rows = att_ref.shape
        attended = att_ref[...].reshape(heads * depth, rows).astype(F32).T.astype(BF16)
        teacher = (patches_ref[...].astype(F32) + scale_ref[...] * dot(attended, proj_ref[...])).astype(BF16)
        through = dot(teacher, head_ref[...], NT)
        wide = teacher.astype(F32)
        seen[...] = (through * lax.rsqrt(jnp.sum(wide * wide, -1, keepdims=True) + eps_norm)).astype(BF16)

    asked = asked_ref[...]
    mine = jnp.sum(jnp.where(lanes(asked.shape) == me_ref[0], asked, 0), -1, keepdims=True)
    hot = jnp.where(lanes((asked.shape[0], seen.shape[0])) == mine - 1, 1.0, 0.0).astype(BF16)
    out_ref[...] = dot(hot, seen[...]).astype(BF16)


def teacher_reply(me, attended, patches, proj, scale, head, asked):
    rows, width = patches.shape
    points = head.shape[0]
    total, devices = asked.shape
    step = total // 6
    return pl.pallas_call(
        teacher_reply_kernel,
        grid_spec=pltpu.PrefetchScalarGridSpec(
            num_scalar_prefetch=1,
            grid=(total // step,),
            in_specs=[
                whole(attended.shape),
                whole((rows, width)),
                whole(proj.shape),
                whole((1, width)),
                whole(head.shape),
                pl.BlockSpec((step, devices), lambda i, m: (i, 0)),
            ],
            out_specs=pl.BlockSpec((step, points), lambda i, m: (i, 0)),
            scratch_shapes=[pltpu.VMEM((rows, points), BF16)],
        ),
        out_shape=jax.ShapeDtypeStruct((total, points), BF16),
        compiler_params=params(),
        cost_estimate=cost(rows * width * (width + points) + total * rows * points, 9 * MIB),
        name="teacher_reply",
    )(me, attended, patches, proj, scale, head, asked)


def request_kernel(tile_ref, patch_ref, place_ref, asked_ref):
    count = tile_ref.shape[0]
    width = 128
    block = 256
    below = jnp.where(
        lanes((block, block)) < lax.broadcasted_iota(jnp.int32, (block, block), 0), 1.0, 0.0
    ).astype(BF16)
    before = jnp.zeros((1, width), F32)
    asked = jnp.zeros((width, width), F32)
    for start in range(0, count, block):
        span = slice(start, start + block)
        tiles = tile_ref[span, :]
        hot = jnp.where(lanes((block, width)) == tiles, 1.0, 0.0)
        earlier = dot(below, hot.astype(BF16)) + before
        before = before + jnp.sum(hot, 0, keepdims=True)
        slot = jnp.sum(earlier * hot, -1, keepdims=True).astype(jnp.int32)
        place_ref[span, :] = tiles * CAP + slot
        slot_hot = jnp.where(lanes((block, width)) == slot, 1.0, 0.0).astype(BF16)
        named = (hot * (patch_ref[span, :] + 1).astype(F32)).astype(BF16)
        asked = asked + dot(slot_hot, named, TN)
    asked_ref[...] = asked[:CAP].astype(jnp.int32)


def requests(tile_ids, patch_ids, devices):
    count = tile_ids.shape[0]
    return pl.pallas_call(
        request_kernel,
        out_shape=(
            jax.ShapeDtypeStruct((count, 1), jnp.int32),
            jax.ShapeDtypeStruct((CAP, devices), jnp.int32),
        ),
        compiler_params=params(),
        cost_estimate=cost(count * 128 * 512, 3 * MIB),
        name="requests",
    )(tile_ids, patch_ids)


def point_mix_kernel(order_ref, feats_ref, gain_ref, w_ref, serial_ref, mix_ref, turned_ref, peak_ref):
    rows, count = order_ref.shape[0], feats_ref.shape[0]
    hot = jnp.where(lanes((rows, count)) == order_ref[...], 1.0, 0.0).astype(BF16)
    serial = dot(hot, feats_ref[...])
    serial_ref[...] = serial.astype(BF16)
    normed = layer_norm(serial, gain_ref[...]).astype(BF16)
    mixed = dot(normed, w_ref[...]).astype(BF16).astype(F32)
    width = w_ref.shape[1]
    scale = jnp.where(lanes((1, width)) < width // 3, HD_P ** (-0.5), 1.0)
    mixed = mixed * scale
    mix_ref[...] = mixed.astype(BF16)
    att = width // 3
    turned_ref[...] = mixed[:, att : 2 * att].T.astype(BF16)
    head = lax.broadcasted_iota(jnp.int32, (att, att), 0) // HD_P
    head_sum = jnp.where(head == lanes((att, att)) // HD_P, 1.0, 0.0).astype(BF16)
    for part in range(2):
        piece = mixed[:, part * att : (part + 1) * att]
        norms = dot((piece * piece).astype(BF16), head_sum)
        peak = jnp.max(norms, 0, keepdims=True)
        peak_ref[:, part * att : (part + 1) * att] = jnp.broadcast_to(peak, (8, att))


def point_mix(order, feats, gain, weights):
    count, width = feats.shape
    step = MIX_STEP
    return pl.pallas_call(
        point_mix_kernel,
        grid=(count // step,),
        in_specs=[
            pl.BlockSpec((step, 1), lambda i: (i, 0)),
            whole((count, width)),
            whole((1, width)),
            whole(weights.shape),
        ],
        out_specs=(
            pl.BlockSpec((step, width), lambda i: (i, 0)),
            pl.BlockSpec((step, weights.shape[1]), lambda i: (i, 0)),
            pl.BlockSpec((weights.shape[1] // 3, step), lambda i: (0, i)),
            pl.BlockSpec((8, 2 * weights.shape[1] // 3), lambda i: (i, 0)),
        ),
        out_shape=(
            jax.ShapeDtypeStruct((count, width), BF16),
            jax.ShapeDtypeStruct((count, weights.shape[1]), BF16),
            jax.ShapeDtypeStruct((weights.shape[1] // 3, count), BF16),
            jax.ShapeDtypeStruct((8 * count // step, 2 * weights.shape[1] // 3), F32),
        ),
        compiler_params=params(),
        cost_estimate=cost(count * width * (count + weights.shape[1]), 9 * MIB),
        name="point_mix",
    )(order, feats, gain, weights)


ROWS = 128
KEYS = 256
GROUP = 128 // HD_P
BOUND = 60.0
PARTS = 4


def window_attention_kernel(
    first,
    base_ref,
    count_ref,
    mix_ref,
    turned_ref,
    peak_ref,
    window_ref,
    out_ref,
    safe,
    query_mark,
    key_mark,
    stack,
    scores,
    top,
    total,
):
    points, width = mix_ref.shape
    att = width // 3
    groups = att // 128
    stacked = GROUP * ROWS

    @pl.when(pl.program_id(0) == 0)
    def _():
        window = window_ref[...]
        slot = lax.broadcasted_iota(jnp.int32, (128, points), 0)
        key_mark[...] = jnp.where((slot < 4) & (slot != window), -BIG, 0.0).astype(BF16)
        same = jnp.where(slot == window, 1.0, 0.0)
        for start in range(0, points, 128):
            query_mark[start : start + 128, :] = same[:, start : start + 128].T.astype(BF16)
        peak = jnp.max(peak_ref[...], 0, keepdims=True)
        safe[0] = (jnp.max(peak[:, :att] * peak[:, att:]) <= BOUND * BOUND).astype(jnp.int32)

    block = pl.program_id(0) + first
    base = base_ref[block]
    steps = count_ref[block]
    here = pl.ds(pl.multiple_of(block * ROWS, ROWS), ROWS)
    lane_head = lanes((ROWS, 128)) // HD_P
    for group in range(groups):
        queries = mix_ref[here, group * 128 : (group + 1) * 128]
        for head in range(GROUP):
            span = slice(group * stacked + head * ROWS, group * stacked + (head + 1) * ROWS)
            stack[span, :128] = jnp.where(lane_head == head, queries, jnp.zeros_like(queries))
            stack[span, 128:] = query_mark[here, :]
    total[...] = jnp.zeros(total.shape, F32)

    def span_of(step, size):
        return pl.ds(pl.multiple_of(base * 128 + step * KEYS, 128), size)

    def keys_of(group, span):
        return jnp.concatenate([turned_ref[group * 128 : (group + 1) * 128, span], key_mark[:, span]], 0)

    def values_of(group, span):
        values = mix_ref[span, 2 * att + group * 128 : 2 * att + (group + 1) * 128]
        return jnp.concatenate([values, jnp.ones_like(values)], 1)

    def fold(step, size):
        span = span_of(step, size)
        rows = stacked // PARTS * 2
        waiting = None
        for group in range(groups):
            keys, values = keys_of(group, span), values_of(group, span)
            for start in range(group * stacked, (group + 1) * stacked, rows):
                part = dot(stack[start : start + rows, :], keys)
                if waiting is not None:
                    total[waiting[0], :] += dot(waiting[1], waiting[2])
                waiting = (slice(start, start + rows), jnp.exp(part).astype(BF16), values)
        total[waiting[0], :] += dot(waiting[1], waiting[2])

    @pl.when(safe[0] == 1)
    def _():
        @pl.loop(0, steps // 2)
        def _(step):
            fold(2 * step, 2 * KEYS)

        @pl.when(steps % 2 == 1)
        def _():
            fold(steps - 1, KEYS)

    @pl.when(safe[0] == 0)
    def _():
        for group in range(groups):
            rows = slice(group * stacked, (group + 1) * stacked)
            top[...] = jnp.full(top.shape, -BIG, F32)

            @pl.loop(0, steps)
            def _(step):
                part = dot(stack[rows, :], keys_of(group, span_of(step, KEYS)))
                scores[step] = part
                top[...] = jnp.maximum(top[...], jnp.maximum(part[:, :128], part[:, 128:]))

            top[...] = jnp.broadcast_to(jnp.max(top[...], -1, keepdims=True), top.shape)

            @pl.loop(0, steps)
            def _(step):
                peak = top[...]
                exps = jnp.exp(scores[step] - jnp.concatenate([peak, peak], 1)).astype(BF16)
                total[rows, :] += dot(exps, values_of(group, span_of(step, KEYS)))

    for group in range(groups):
        attended = jnp.zeros((ROWS, 128), F32)
        for head in range(GROUP):
            span = slice(group * stacked + head * ROWS, group * stacked + (head + 1) * ROWS)
            attended = jnp.where(lane_head == head, total[span, :128] / total[span, 128:], attended)
        out_ref[:, group * 128 : (group + 1) * 128] = attended.astype(BF16)


def window_ranges(windows):
    points = windows.shape[0]
    blocks = windows.reshape(points // ROWS, ROWS)
    start = jnp.sum((windows[None, :] < blocks[:, :1]).astype(jnp.int32), 1)
    end = jnp.sum((windows[None, :] <= blocks[:, -1:]).astype(jnp.int32), 1)
    base = start // 128
    count = (end - base * 128 + KEYS - 1) // KEYS
    base = jnp.minimum(base, points // 128 - count * (KEYS // 128))
    return base, count


def window_attention(mix, turned, peaks, window_row, base, count, first, blocks):
    points, width = mix.shape
    att = width // 3
    stacked = GROUP * ROWS
    return pl.pallas_call(
        functools.partial(window_attention_kernel, first),
        grid_spec=pltpu.PrefetchScalarGridSpec(
            num_scalar_prefetch=2,
            grid=(blocks,),
            in_specs=[whole((points, width)), whole((att, points)), whole(peaks.shape), whole((1, points))],
            out_specs=pl.BlockSpec((ROWS, att), lambda i, b, c: (i, 0)),
            scratch_shapes=[
                pltpu.SMEM((1,), jnp.int32),
                pltpu.VMEM((points, 128), BF16),
                pltpu.VMEM((128, points), BF16),
                pltpu.VMEM((att // 128 * stacked, 256), BF16),
                pltpu.VMEM((points // KEYS, stacked, KEYS), F32),
                pltpu.VMEM((stacked, 128), F32),
                pltpu.VMEM((att // 128 * stacked, 256), F32),
            ],
        ),
        out_shape=jax.ShapeDtypeStruct((blocks * ROWS, att), BF16),
        compiler_params=params(),
        cost_estimate=cost(
            blocks * ROWS * 1024 * 16 * 512, 5 * MIB, blocks * ROWS * 1024 * 16
        ),
        name="window_attention",
    )(base, count, mix, turned, peaks, window_row)


def point_block_kernel(serial_ref, att_ref, proj_ref, gain_ref, up_ref, down_ref, head_ref, out_ref, norm_ref):
    residual = serial_ref[...].astype(F32) + dot(att_ref[...], proj_ref[...])
    normed = layer_norm(residual, gain_ref[...]).astype(BF16)
    hidden_width = up_ref.shape[1]
    chunk = HIDDEN
    added = None
    for start in range(0, hidden_width, chunk):
        before = dot(normed, up_ref[:, start : start + chunk])
        hidden = (0.5 * before * (1.0 + lax.erf(before * (0.5**0.5)))).astype(BF16)
        part = dot(hidden, down_ref[start : start + chunk, :])
        added = part if added is None else added + part
    block_out = (residual + added).astype(BF16)
    out_ref[...] = block_out
    student = dot(block_out, head_ref[...])
    norm_ref[...] = jnp.sum(student * student, -1, keepdims=True)


def point_block(serial, attended, proj, gain, up, down, head):
    count, width = serial.shape
    att = attended.shape[1]
    step = BLOCK_STEP
    return pl.pallas_call(
        point_block_kernel,
        grid=(count // step,),
        in_specs=[
            pl.BlockSpec((step, width), lambda i: (i, 0)),
            pl.BlockSpec((step, att), lambda i: (i, 0)),
            whole(proj.shape),
            whole((1, width)),
            whole(up.shape),
            whole(down.shape),
            whole(head.shape),
        ],
        out_specs=(
            pl.BlockSpec((step, width), lambda i: (i, 0)),
            pl.BlockSpec((step, 1), lambda i: (i, 0)),
        ),
        out_shape=(
            jax.ShapeDtypeStruct((count, width), BF16),
            jax.ShapeDtypeStruct((count, 1), F32),
        ),
        compiler_params=params(),
        cost_estimate=cost(
            count * width * (att + 2 * up.shape[1] + head.shape[1]), 12 * MIB, count * up.shape[1]
        ),
        name="point_block",
    )(serial, attended, proj, gain, up, down, head)


def loss_kernel(place_ref, out_ref, norm_ref, replies_ref, loss_ref):
    rows, total = place_ref.shape[0], replies_ref.shape[0]
    hot = jnp.where(lanes((rows, total)) == place_ref[...], 1.0, 0.0).astype(BF16)
    target = dot(hot, replies_ref[...])
    inner = jnp.sum(out_ref[...].astype(F32) * target, -1, keepdims=True)
    loss_ref[...] = 1.0 - inner * lax.rsqrt(norm_ref[...] + eps_norm)


def loss(place, point_out, norms, replies):
    count, width = point_out.shape
    step = LOSS_STEP
    return pl.pallas_call(
        loss_kernel,
        grid=(count // step,),
        in_specs=[
            pl.BlockSpec((step, 1), lambda i: (i, 0)),
            pl.BlockSpec((step, width), lambda i: (i, 0)),
            pl.BlockSpec((step, 1), lambda i: (i, 0)),
            whole(replies.shape),
        ],
        out_specs=pl.BlockSpec((step, 1), lambda i: (i, 0)),
        out_shape=jax.ShapeDtypeStruct((count, 1), F32),
        compiler_params=params(),
        cost_estimate=cost(count * width * replies.shape[0], 8 * MIB),
        name="loss",
    )(place, point_out, norms, replies)


def local(
    patches,
    vit_gain,
    vit_qkv,
    vit_qkv_bias,
    vit_proj,
    vit_scale,
    point_feats,
    point_order,
    window_ids,
    point_tile,
    point_patch,
    pt_gain,
    pt_qkv,
    pt_proj,
    pt_up,
    pt_down,
    head_w,
):
    both = ("cam", "tile")
    tile_count = lax.axis_size("tile")
    device_count = lax.axis_size("cam") * tile_count
    tile_index = lax.axis_index("tile")
    me = (lax.axis_index("cam") * tile_count + tile_index).astype(jnp.int32).reshape(1)
    core = (tile_index % 2).astype(jnp.int32).reshape(1)
    count = point_feats.shape[0]

    mix = teacher_mix(patches[0], vit_gain[None], vit_qkv, vit_qkv_bias[None])
    mix = lax.all_to_all(mix, "tile", split_axis=0, concat_axis=0, tiled=True)

    place, asked = requests(point_tile, point_patch[:, None], device_count)
    asked = lax.all_gather(asked, both, axis=0, tiled=True)
    serial, pt_mix, pt_turned, peaks = point_mix(
        point_order.reshape(count, 1), point_feats, pt_gain[:1], pt_qkv
    )
    base, steps = window_ranges(window_ids[0])
    blocks = count // ROWS
    cuts = (0, blocks // 4, blocks // 2, blocks)

    def attend(part, base):
        return window_attention(
            pt_mix, pt_turned, peaks, window_ids, base, steps, cuts[part], cuts[part + 1] - cuts[part]
        )

    parts = [attend(0, base)]
    mix, parts[0] = lax.optimization_barrier((mix, parts[0]))
    attended = teacher_attention(core, mix)
    groups = [[2 * i + c for i in range(tile_count // 2)] for c in range(2)]
    attended, base = lax.optimization_barrier((attended, base))
    attended = lax.all_to_all(
        attended, "tile", split_axis=0, concat_axis=0, tiled=True, axis_index_groups=groups
    )
    parts.append(attend(1, base))
    attended, parts[1], base = lax.optimization_barrier((attended, parts[1], base))
    replies = teacher_reply(me, attended, patches[0], vit_proj, vit_scale[None], head_w, asked)
    replies, base = lax.optimization_barrier((replies, base))
    replies = lax.all_to_all(
        replies.reshape(device_count, CAP, -1), both, split_axis=0, concat_axis=0, tiled=True
    ).reshape(device_count * CAP, -1)
    parts.append(attend(2, base))
    pt_attended = jnp.concatenate(parts, 0)
    point_out, norms = point_block(serial, pt_attended, pt_proj, pt_gain[1:], pt_up, pt_down, head_w)
    losses = loss(place, point_out, norms, replies)
    return (point_out, losses.reshape(count))


def solution(mesh):
    both = ("cam", "tile")
    placed = (
        P("cam", "tile", None),
        P(),
        P(),
        P(),
        P(),
        P(),
        P(both, None),
        P(both, None),
        P(both, None),
        P(both, None),
        P(both),
        P(),
        P(),
        P(),
        P(),
        P(),
        P(),
    )
    return jax.shard_map(
        local,
        mesh=mesh,
        in_specs=placed,
        out_specs=(P(both, None), P(both)),
        check_vma=False,
    )
```

```python
import functools

import jax
import jax.numpy as jnp
from jax import lax
from jax.experimental import pallas as pl
from jax.experimental.pallas import tpu as pltpu
from jax.sharding import PartitionSpec as P

HD_V = 64
HD_P = 16
CAP = 24
eps_norm = 1e-06
BIG = 1e30
MIB = 1024 * 1024
F32 = jnp.float32
BF16 = jnp.bfloat16
NT = (((1,), (1,)), ((), ()))
TN = (((0,), (0,)), ((), ()))
MIX_STEP = 512
BLOCK_STEP = 512
HIDDEN = 512
LOSS_STEP = 512


def layer_norm(values, gain):
    center = values - jnp.mean(values, -1, keepdims=True)
    spread = jnp.mean(center * center, -1, keepdims=True)
    return center * lax.rsqrt(spread + eps_norm) * gain


def dot(left, right, dims=None):
    if dims is None:
        return jnp.dot(left, right, preferred_element_type=F32)
    return lax.dot_general(left, right, dims, preferred_element_type=F32)


def lanes(shape):
    return lax.broadcasted_iota(jnp.int32, shape, len(shape) - 1)


def column(row):
    pieces = []
    for start in range(0, row.shape[1], 128):
        own = lanes((128, 128)) == lax.broadcasted_iota(jnp.int32, (128, 128), 0)
        pieces.append(jnp.sum(jnp.where(own, row[:, start : start + 128], 0), 1, keepdims=True))
    return jnp.concatenate(pieces, 0)


def row_of(col):
    pieces = []
    for start in range(0, col.shape[0], 128):
        own = lanes((128, 128)) == lax.broadcasted_iota(jnp.int32, (128, 128), 0)
        pieces.append(jnp.sum(jnp.where(own, col[start : start + 128], 0), 0, keepdims=True))
    return jnp.concatenate(pieces, 1)


def whole(shape):
    return pl.BlockSpec(shape, lambda *_: (0,) * len(shape))


def params(limit):
    return pltpu.CompilerParams(vmem_limit_bytes=limit * MIB)


def cost(macs, moved, exps=0):
    return pl.CostEstimate(flops=2 * macs, bytes_accessed=moved, transcendentals=exps)


def teacher_mix_kernel(x_ref, gain_ref, wq_ref, wk_ref, wv_ref, bq_ref, bk_ref, bv_ref, out_ref, normed):
    @pl.when(pl.program_id(0) == 0)
    def _():
        normed[...] = layer_norm(x_ref[...].astype(F32), gain_ref[...]).astype(BF16)

    rows = normed[...]
    for part, (w_ref, b_ref) in enumerate(((wq_ref, bq_ref), (wk_ref, bk_ref), (wv_ref, bv_ref))):
        mixed = (dot(rows, w_ref[...]) + b_ref[...]).astype(BF16).astype(F32)
        if part == 0:
            mixed = mixed * HD_V ** (-0.5)
        turned = mixed.T.astype(BF16)
        for head in range(turned.shape[0] // HD_V):
            piece = turned[head * HD_V : (head + 1) * HD_V]
            for core in range(2):
                out_ref[2 * head + core, part * HD_V : (part + 1) * HD_V, :] = piece


def teacher_mix(patches, gain, weights, bias):
    rows, width = patches.shape
    heads = width // HD_V
    step = 256
    steps = width // step

    def col(part):
        return pl.BlockSpec((width, step), lambda i: (0, part * steps + i))

    def bias_col(part):
        return pl.BlockSpec((1, step), lambda i: (0, part * steps + i))

    return pl.pallas_call(
        teacher_mix_kernel,
        grid=(steps,),
        in_specs=[whole((rows, width)), whole((1, width))]
        + [col(p) for p in range(3)]
        + [bias_col(p) for p in range(3)],
        out_specs=pl.BlockSpec((2 * step // HD_V, 3 * HD_V, rows), lambda i: (i, 0, 0)),
        out_shape=jax.ShapeDtypeStruct((2 * heads, 3 * HD_V, rows), BF16),
        scratch_shapes=[pltpu.VMEM((rows, width), BF16)],
        compiler_params=params(16),
        cost_estimate=cost(rows * width * 3 * width, 8 * MIB),
        name="teacher_mix",
    )(patches, gain, weights, weights, weights, bias, bias, bias)


BOUND = 60.0
TILES = 4


def teacher_attention_kernel(core_ref, mix_ref, out_ref, safe, keys, values, scores):
    tiles, _, rows = mix_ref.shape
    step = pl.program_id(0)
    core = core_ref[0]
    count = tiles * rows

    @pl.when(step == 0)
    def _():
        peaks = [None, None]
        for tile in range(tiles):
            span = slice(tile * rows, (tile + 1) * rows)
            keys[:, span] = mix_ref[tile, HD_V : 2 * HD_V, :]
            turned = mix_ref[tile, 2 * HD_V :, :].astype(F32)
            values[span, :] = jnp.concatenate([turned, jnp.ones_like(turned)], 0).T.astype(BF16)
            for part in range(2):
                piece = mix_ref[tile, part * HD_V : (part + 1) * HD_V, :].astype(F32)
                norms = jnp.sum(piece * piece, 0, keepdims=True)
                peaks[part] = norms if peaks[part] is None else jnp.maximum(peaks[part], norms)
        bound = jnp.max(peaks[0], -1, keepdims=True) * jnp.max(peaks[1], -1, keepdims=True)
        safe[0] = (jnp.max(bound) <= BOUND * BOUND).astype(jnp.int32)

    first = TILES * step
    queries = [mix_ref[2 * (first + i) + core, :HD_V, :].astype(F32) for i in range(TILES)]
    queries = jnp.concatenate(queries, 1).T.astype(BF16)

    def finish(total):
        turned = total.T
        attended = (turned[:HD_V] / turned[HD_V:]).astype(BF16)
        for i in range(TILES):
            out_ref[i] = attended[:, i * rows : (i + 1) * rows]

    @pl.when(safe[0] == 1)
    def _():
        chunk = 512
        total, waiting = None, None
        for start in list(range(0, count, chunk)) + [None]:
            part = None if start is None else dot(queries, keys[:, start : start + chunk])
            if waiting is not None:
                added = dot(waiting[1], values[waiting[0] : waiting[0] + chunk, :])
                total = added if total is None else total + added
            if start is not None:
                waiting = (start, jnp.exp(part).astype(BF16))
        finish(total)

    @pl.when(safe[0] == 0)
    def _():
        chunk = 1024
        top = None
        for start in range(0, count, chunk):
            part = dot(queries, keys[:, start : start + chunk])
            scores[:, start : start + chunk] = part
            peak = jnp.max(part, -1, keepdims=True)
            top = peak if top is None else jnp.maximum(top, peak)
        total = None
        for start in range(0, count, chunk):
            exps = jnp.exp(scores[:, start : start + chunk] - top).astype(BF16)
            part = dot(exps, values[start : start + chunk, :])
            total = part if total is None else total + part
        finish(total)


def teacher_attention(core, mix):
    tiles, depth, rows = mix.shape
    return pl.pallas_call(
        teacher_attention_kernel,
        grid_spec=pltpu.PrefetchScalarGridSpec(
            num_scalar_prefetch=1,
            grid=(tiles // 2 // TILES,),
            in_specs=[whole((tiles, depth, rows))],
            out_specs=pl.BlockSpec((TILES, HD_V, rows), lambda i, c: (i, 0, 0)),
            scratch_shapes=[
                pltpu.SMEM((1,), jnp.int32),
                pltpu.VMEM((HD_V, tiles * rows), BF16),
                pltpu.VMEM((tiles * rows, 128), BF16),
                pltpu.VMEM((TILES * rows, tiles * rows), F32),
            ],
        ),
        out_shape=jax.ShapeDtypeStruct((tiles // 2, HD_V, rows), BF16),
        compiler_params=params(28),
        cost_estimate=cost(2 * tiles * rows * tiles * rows * 128, 2 * MIB, tiles * rows * tiles * rows // 2),
        name="teacher_attention",
    )(core, mix)


def teacher_reply_kernel(me_ref, att_ref, patches_ref, proj_ref, scale_ref, head_ref, asked_ref, out_ref, seen):
    @pl.when(pl.program_id(0) == 0)
    def _():
        heads, depth, rows = att_ref.shape
        attended = att_ref[...].reshape(heads * depth, rows).astype(F32).T.astype(BF16)
        teacher = (patches_ref[...].astype(F32) + scale_ref[...] * dot(attended, proj_ref[...])).astype(BF16)
        through = dot(teacher, head_ref[...], NT)
        wide = teacher.astype(F32)
        seen[...] = (through * lax.rsqrt(jnp.sum(wide * wide, -1, keepdims=True) + eps_norm)).astype(BF16)

    asked = asked_ref[...]
    mine = jnp.sum(jnp.where(lanes(asked.shape) == me_ref[0], asked, 0), -1, keepdims=True)
    hot = jnp.where(lanes((asked.shape[0], seen.shape[0])) == mine - 1, 1.0, 0.0).astype(BF16)
    out_ref[...] = dot(hot, seen[...]).astype(BF16)


def teacher_reply(me, attended, patches, proj, scale, head, asked):
    rows, width = patches.shape
    points = head.shape[0]
    total, devices = asked.shape
    step = total // 6
    return pl.pallas_call(
        teacher_reply_kernel,
        grid_spec=pltpu.PrefetchScalarGridSpec(
            num_scalar_prefetch=1,
            grid=(total // step,),
            in_specs=[
                whole(attended.shape),
                whole((rows, width)),
                whole(proj.shape),
                whole((1, width)),
                whole(head.shape),
                pl.BlockSpec((step, devices), lambda i, m: (i, 0)),
            ],
            out_specs=pl.BlockSpec((step, points), lambda i, m: (i, 0)),
            scratch_shapes=[pltpu.VMEM((rows, points), BF16)],
        ),
        out_shape=jax.ShapeDtypeStruct((total, points), BF16),
        compiler_params=params(24),
        cost_estimate=cost(rows * width * (width + points) + total * rows * points, 9 * MIB),
        name="teacher_reply",
    )(me, attended, patches, proj, scale, head, asked)


def request_kernel(tile_ref, patch_ref, place_ref, asked_ref):
    count = tile_ref.shape[1]
    width = asked_ref.shape[1]
    block = 256
    earlier_than = jnp.where(
        lax.broadcasted_iota(jnp.int32, (block, block), 0) < lanes((block, block)), 1.0, 0.0
    ).astype(BF16)
    before = jnp.zeros((width, 1), F32)
    asked = jnp.zeros((32, width), F32)
    for start in range(0, count, block):
        span = slice(start, start + block)
        tiles = tile_ref[:, span]
        hot = jnp.where(lax.broadcasted_iota(jnp.int32, (width, block), 0) == tiles, 1.0, 0.0)
        earlier = dot(hot.astype(BF16), earlier_than) + before
        before = before + jnp.sum(hot, 1, keepdims=True)
        slot = jnp.sum(earlier * hot, 0, keepdims=True).astype(jnp.int32)
        place_ref[:, span] = tiles * CAP + slot
        slot_hot = jnp.where(lax.broadcasted_iota(jnp.int32, (32, block), 0) == slot, 1.0, 0.0)
        named = (hot * (patch_ref[:, span] + 1).astype(F32)).astype(BF16)
        asked = asked + dot(slot_hot.astype(BF16), named, NT)
    asked_ref[...] = asked[:CAP].astype(jnp.int32)


def requests(tile_ids, patch_ids, devices):
    count = tile_ids.shape[1]
    return pl.pallas_call(
        request_kernel,
        out_shape=(
            jax.ShapeDtypeStruct((1, count), jnp.int32),
            jax.ShapeDtypeStruct((CAP, devices), jnp.int32),
        ),
        compiler_params=params(12),
        cost_estimate=cost(count * 128 * 512, MIB),
        name="requests",
    )(tile_ids, patch_ids)


def point_mix_kernel(order_ref, feats_ref, gain_ref, w_ref, serial_ref, mix_ref, turned_ref, peak_ref):
    rows, count = order_ref.shape[1], feats_ref.shape[0]
    hot = jnp.where(lanes((rows, count)) == column(order_ref[...]), 1.0, 0.0).astype(BF16)
    serial = dot(hot, feats_ref[...])
    serial_ref[...] = serial.astype(BF16)
    normed = layer_norm(serial, gain_ref[...]).astype(BF16)
    mixed = dot(normed, w_ref[...]).astype(BF16).astype(F32)
    width = w_ref.shape[1]
    scale = jnp.where(lanes((1, width)) < width // 3, HD_P ** (-0.5), 1.0)
    mixed = mixed * scale
    mix_ref[...] = mixed.astype(BF16)
    att = width // 3
    turned_ref[...] = mixed[:, att : 2 * att].T.astype(BF16)
    head = lax.broadcasted_iota(jnp.int32, (att, att), 0) // HD_P
    head_sum = jnp.where(head == lanes((att, att)) // HD_P, 1.0, 0.0).astype(BF16)
    for part in range(2):
        piece = mixed[:, part * att : (part + 1) * att]
        norms = dot((piece * piece).astype(BF16), head_sum)
        peak = jnp.max(norms, 0, keepdims=True)
        peak_ref[:, part * att : (part + 1) * att] = jnp.broadcast_to(peak, (8, att))


def point_mix(order, feats, gain, weights):
    count, width = feats.shape
    step = MIX_STEP
    return pl.pallas_call(
        point_mix_kernel,
        grid=(count // step,),
        in_specs=[
            pl.BlockSpec((1, step), lambda i: (0, i)),
            whole((count, width)),
            whole((1, width)),
            whole(weights.shape),
        ],
        out_specs=(
            pl.BlockSpec((step, width), lambda i: (i, 0)),
            pl.BlockSpec((step, weights.shape[1]), lambda i: (i, 0)),
            pl.BlockSpec((weights.shape[1] // 3, step), lambda i: (0, i)),
            pl.BlockSpec((8, 2 * weights.shape[1] // 3), lambda i: (i, 0)),
        ),
        out_shape=(
            jax.ShapeDtypeStruct((count, width), BF16),
            jax.ShapeDtypeStruct((count, weights.shape[1]), BF16),
            jax.ShapeDtypeStruct((weights.shape[1] // 3, count), BF16),
            jax.ShapeDtypeStruct((8 * count // step, 2 * weights.shape[1] // 3), F32),
        ),
        compiler_params=params(28),
        cost_estimate=cost(count * width * (count + weights.shape[1]), 9 * MIB),
        name="point_mix",
    )(order, feats, gain, weights)


ROWS = 128
KEYS = 256
GROUP = 128 // HD_P
PARTS = 4


def window_attention_kernel(
    first,
    base_ref,
    count_ref,
    mix_ref,
    turned_ref,
    peak_ref,
    window_ref,
    out_ref,
    safe,
    query_mark,
    key_mark,
    stack,
    top,
    total,
):
    points, width = mix_ref.shape
    att = width // 3
    groups = att // 128
    stacked = GROUP * ROWS

    @pl.when(pl.program_id(0) == 0)
    def _():
        window = window_ref[...]
        slot = lax.broadcasted_iota(jnp.int32, (128, points), 0)
        key_mark[...] = jnp.where((slot < 4) & (slot != window), -BIG, 0.0).astype(BF16)
        same = jnp.where(slot == window, 1.0, 0.0)
        for start in range(0, points, 128):
            query_mark[start : start + 128, :] = same[:, start : start + 128].T.astype(BF16)
        peak = jnp.max(peak_ref[...], 0, keepdims=True)
        safe[0] = (jnp.max(peak[:, :att] * peak[:, att:]) <= BOUND * BOUND).astype(jnp.int32)

    block = pl.program_id(0) + first
    base = base_ref[block]
    steps = count_ref[block]
    here = pl.ds(pl.multiple_of(block * ROWS, ROWS), ROWS)
    lane_head = lanes((ROWS, 128)) // HD_P
    for group in range(groups):
        queries = mix_ref[here, group * 128 : (group + 1) * 128]
        for head in range(GROUP):
            span = slice(group * stacked + head * ROWS, group * stacked + (head + 1) * ROWS)
            stack[span, :128] = jnp.where(lane_head == head, queries, jnp.zeros_like(queries))
            stack[span, 128:] = query_mark[here, :]
    total[...] = jnp.zeros(total.shape, F32)

    def span_of(step, size):
        return pl.ds(pl.multiple_of(base * 128 + step * KEYS, 128), size)

    def keys_of(group, span):
        return jnp.concatenate([turned_ref[group * 128 : (group + 1) * 128, span], key_mark[:, span]], 0)

    def values_of(group, span):
        values = mix_ref[span, 2 * att + group * 128 : 2 * att + (group + 1) * 128]
        return jnp.concatenate([values, jnp.ones_like(values)], 1)

    def fold(step, size):
        span = span_of(step, size)
        rows = stacked // PARTS * 2
        waiting = None
        for group in range(groups):
            keys, values = keys_of(group, span), values_of(group, span)
            for start in range(group * stacked, (group + 1) * stacked, rows):
                part = dot(stack[start : start + rows, :], keys)
                if waiting is not None:
                    total[waiting[0], :] += dot(waiting[1], waiting[2])
                waiting = (slice(start, start + rows), jnp.exp(part).astype(BF16), values)
        total[waiting[0], :] += dot(waiting[1], waiting[2])

    @pl.when(safe[0] == 1)
    def _():
        @pl.loop(0, steps // 2)
        def _(step):
            fold(2 * step, 2 * KEYS)

        @pl.when(steps % 2 == 1)
        def _():
            fold(steps - 1, KEYS)

    @pl.when(safe[0] == 0)
    def _():
        for group in range(groups):
            rows = slice(group * stacked, (group + 1) * stacked)
            top[...] = jnp.full(top.shape, -BIG, F32)

            @pl.loop(0, steps)
            def _(step):
                part = dot(stack[rows, :], keys_of(group, span_of(step, KEYS)))
                top[...] = jnp.maximum(top[...], jnp.maximum(part[:, :128], part[:, 128:]))

            top[...] = jnp.broadcast_to(jnp.max(top[...], -1, keepdims=True), top.shape)

            @pl.loop(0, steps)
            def _(step):
                span = span_of(step, KEYS)
                part = dot(stack[rows, :], keys_of(group, span))
                peak = top[...]
                exps = jnp.exp(part - jnp.concatenate([peak, peak], 1)).astype(BF16)
                total[rows, :] += dot(exps, values_of(group, span))

    for group in range(groups):
        attended = jnp.zeros((ROWS, 128), F32)
        for head in range(GROUP):
            span = slice(group * stacked + head * ROWS, group * stacked + (head + 1) * ROWS)
            attended = jnp.where(lane_head == head, total[span, :128] / total[span, 128:], attended)
        out_ref[:, group * 128 : (group + 1) * 128] = attended.astype(BF16)


def window_ranges(windows):
    points = windows.shape[0]
    blocks = windows.reshape(points // ROWS, ROWS)
    start = jnp.sum((windows[None, :] < blocks[:, :1]).astype(jnp.int32), 1)
    end = jnp.sum((windows[None, :] <= blocks[:, -1:]).astype(jnp.int32), 1)
    base = start // 128
    count = (end - base * 128 + KEYS - 1) // KEYS
    base = jnp.minimum(base, points // 128 - count * (KEYS // 128))
    return base, count


def window_attention(mix, turned, peaks, window_row, base, count, first, blocks):
    points, width = mix.shape
    att = width // 3
    stacked = GROUP * ROWS
    return pl.pallas_call(
        functools.partial(window_attention_kernel, first),
        grid_spec=pltpu.PrefetchScalarGridSpec(
            num_scalar_prefetch=2,
            grid=(blocks,),
            in_specs=[whole((points, width)), whole((att, points)), whole(peaks.shape), whole((1, points))],
            out_specs=pl.BlockSpec((ROWS, att), lambda i, b, c: (i, 0)),
            scratch_shapes=[
                pltpu.SMEM((1,), jnp.int32),
                pltpu.VMEM((points, 128), BF16),
                pltpu.VMEM((128, points), BF16),
                pltpu.VMEM((att // 128 * stacked, 256), BF16),
                pltpu.VMEM((stacked, 128), F32),
                pltpu.VMEM((att // 128 * stacked, 256), F32),
            ],
        ),
        out_shape=jax.ShapeDtypeStruct((blocks * ROWS, att), BF16),
        compiler_params=params(28),
        cost_estimate=cost(
            blocks * ROWS * 1024 * 16 * 512, 5 * MIB, blocks * ROWS * 1024 * 16
        ),
        name="window_attention",
    )(base, count, mix, turned, peaks, window_row)


def point_block_kernel(serial_ref, att_ref, proj_ref, gain_ref, up_ref, down_ref, head_ref, out_ref, norm_ref):
    residual = serial_ref[...].astype(F32) + dot(att_ref[...], proj_ref[...])
    normed = layer_norm(residual, gain_ref[...]).astype(BF16)
    hidden_width = up_ref.shape[1]
    chunk = HIDDEN
    added = None
    for start in range(0, hidden_width, chunk):
        before = dot(normed, up_ref[:, start : start + chunk])
        hidden = (0.5 * before * (1.0 + lax.erf(before * (0.5**0.5)))).astype(BF16)
        part = dot(hidden, down_ref[start : start + chunk, :])
        added = part if added is None else added + part
    block_out = (residual + added).astype(BF16)
    out_ref[...] = block_out
    student = dot(block_out, head_ref[...])
    norm_ref[...] = jnp.sum(student * student, -1, keepdims=True)


def point_block(serial, attended, proj, gain, up, down, head):
    count, width = serial.shape
    att = attended.shape[1]
    step = BLOCK_STEP
    return pl.pallas_call(
        point_block_kernel,
        grid=(count // step,),
        in_specs=[
            pl.BlockSpec((step, width), lambda i: (i, 0)),
            pl.BlockSpec((step, att), lambda i: (i, 0)),
            whole(proj.shape),
            whole((1, width)),
            whole(up.shape),
            whole(down.shape),
            whole(head.shape),
        ],
        out_specs=(
            pl.BlockSpec((step, width), lambda i: (i, 0)),
            pl.BlockSpec((step, 1), lambda i: (i, 0)),
        ),
        out_shape=(
            jax.ShapeDtypeStruct((count, width), BF16),
            jax.ShapeDtypeStruct((count, 1), F32),
        ),
        compiler_params=params(36),
        cost_estimate=cost(
            count * width * (att + 2 * up.shape[1] + head.shape[1]), 12 * MIB, count * up.shape[1]
        ),
        name="point_block",
    )(serial, attended, proj, gain, up, down, head)


def loss_kernel(place_ref, out_ref, norm_ref, replies_ref, loss_ref):
    rows, total = place_ref.shape[1], replies_ref.shape[0]
    hot = jnp.where(lanes((rows, total)) == column(place_ref[...]), 1.0, 0.0).astype(BF16)
    target = dot(hot, replies_ref[...])
    inner = jnp.sum(out_ref[...].astype(F32) * target, -1, keepdims=True)
    loss_ref[...] = 1.0 - row_of(inner * lax.rsqrt(norm_ref[...] + eps_norm))


def loss(place, point_out, norms, replies):
    count, width = point_out.shape
    step = LOSS_STEP
    return pl.pallas_call(
        loss_kernel,
        grid=(count // step,),
        in_specs=[
            pl.BlockSpec((1, step), lambda i: (0, i)),
            pl.BlockSpec((step, width), lambda i: (i, 0)),
            pl.BlockSpec((step, 1), lambda i: (i, 0)),
            whole(replies.shape),
        ],
        out_specs=pl.BlockSpec((1, step), lambda i: (0, i)),
        out_shape=jax.ShapeDtypeStruct((1, count), F32),
        compiler_params=params(32),
        cost_estimate=cost(count * width * replies.shape[0], 8 * MIB),
        name="loss",
    )(place, point_out, norms, replies)


def local(
    patches,
    vit_gain,
    vit_qkv,
    vit_qkv_bias,
    vit_proj,
    vit_scale,
    point_feats,
    point_order,
    window_ids,
    point_tile,
    point_patch,
    pt_gain,
    pt_qkv,
    pt_proj,
    pt_up,
    pt_down,
    head_w,
):
    both = ("cam", "tile")
    tile_count = lax.axis_size("tile")
    device_count = lax.axis_size("cam") * tile_count
    tile_index = lax.axis_index("tile")
    me = (lax.axis_index("cam") * tile_count + tile_index).astype(jnp.int32).reshape(1)
    core = (tile_index % 2).astype(jnp.int32).reshape(1)
    count = point_feats.shape[0]

    mix = teacher_mix(patches[0], vit_gain[None], vit_qkv, vit_qkv_bias[None])
    mix = lax.all_to_all(mix, "tile", split_axis=0, concat_axis=0, tiled=True)

    place, asked = requests(point_tile.reshape(1, count), point_patch.reshape(1, count), device_count)
    asked = lax.all_gather(asked, both, axis=0, tiled=True)
    serial, pt_mix, pt_turned, peaks = point_mix(
        point_order, point_feats, pt_gain[:1], pt_qkv
    )
    base, steps = window_ranges(window_ids[0])
    blocks = count // ROWS
    cuts = (0, 3 * blocks // 16, 3 * blocks // 8, blocks)

    def attend(part, base):
        return window_attention(
            pt_mix, pt_turned, peaks, window_ids, base, steps, cuts[part], cuts[part + 1] - cuts[part]
        )

    parts = [attend(0, base)]
    mix, parts[0] = lax.optimization_barrier((mix, parts[0]))
    attended = teacher_attention(core, mix)
    groups = [[2 * i + c for i in range(tile_count // 2)] for c in range(2)]
    attended, base = lax.optimization_barrier((attended, base))
    attended = lax.all_to_all(
        attended, "tile", split_axis=0, concat_axis=0, tiled=True, axis_index_groups=groups
    )
    parts.append(attend(1, base))
    attended, parts[1], base = lax.optimization_barrier((attended, parts[1], base))
    replies = teacher_reply(me, attended, patches[0], vit_proj, vit_scale[None], head_w, asked)
    replies, base = lax.optimization_barrier((replies, base))
    replies = lax.all_to_all(
        replies.reshape(device_count, CAP, -1), both, split_axis=0, concat_axis=0, tiled=True
    ).reshape(device_count * CAP, -1)
    parts.append(attend(2, base))
    pt_attended = jnp.concatenate(parts, 0)
    point_out, norms = point_block(serial, pt_attended, pt_proj, pt_gain[1:], pt_up, pt_down, head_w)
    losses = loss(place, point_out, norms, replies)
    return (point_out, losses.reshape(count))


def solution(mesh):
    both = ("cam", "tile")
    placed = (
        P("cam", "tile", None),
        P(),
        P(),
        P(),
        P(),
        P(),
        P(both, None),
        P(both, None),
        P(both, None),
        P(both, None),
        P(both),
        P(),
        P(),
        P(),
        P(),
        P(),
        P(),
    )
    return jax.shard_map(
        local,
        mesh=mesh,
        in_specs=placed,
        out_specs=(P(both, None), P(both)),
        check_vma=False,
    )
```

```python
import functools

import jax
import jax.numpy as jnp
from jax import lax
from jax.experimental import pallas as pl
from jax.experimental.pallas import tpu as pltpu
from jax.sharding import PartitionSpec as P

HD_V = 64
HD_P = 16
CAP = 24
eps_norm = 1e-06
BIG = 1e30
MIB = 1024 * 1024
F32 = jnp.float32
BF16 = jnp.bfloat16
NT = (((1,), (1,)), ((), ()))
TN = (((0,), (0,)), ((), ()))
MIX_STEP = 512
BLOCK_STEP = 512
HIDDEN = 512
LOSS_STEP = 512


def layer_norm(values, gain):
    center = values - jnp.mean(values, -1, keepdims=True)
    spread = jnp.mean(center * center, -1, keepdims=True)
    return center * lax.rsqrt(spread + eps_norm) * gain


def dot(left, right, dims=None):
    if dims is None:
        return jnp.dot(left, right, preferred_element_type=F32)
    return lax.dot_general(left, right, dims, preferred_element_type=F32)


def lanes(shape):
    return lax.broadcasted_iota(jnp.int32, shape, len(shape) - 1)


def column(row):
    pieces = []
    for start in range(0, row.shape[1], 128):
        own = lanes((128, 128)) == lax.broadcasted_iota(jnp.int32, (128, 128), 0)
        pieces.append(jnp.sum(jnp.where(own, row[:, start : start + 128], 0), 1, keepdims=True))
    return jnp.concatenate(pieces, 0)


def row_of(col):
    pieces = []
    for start in range(0, col.shape[0], 128):
        own = lanes((128, 128)) == lax.broadcasted_iota(jnp.int32, (128, 128), 0)
        pieces.append(jnp.sum(jnp.where(own, col[start : start + 128], 0), 0, keepdims=True))
    return jnp.concatenate(pieces, 1)


def whole(shape):
    return pl.BlockSpec(shape, lambda *_: (0,) * len(shape))


def params(limit):
    return pltpu.CompilerParams(vmem_limit_bytes=limit * MIB)


def cost(macs, moved, exps=0):
    return pl.CostEstimate(flops=2 * macs, bytes_accessed=moved, transcendentals=exps)


def teacher_mix_kernel(x_ref, gain_ref, wq_ref, wk_ref, wv_ref, bq_ref, bk_ref, bv_ref, out_ref, normed):
    @pl.when(pl.program_id(0) == 0)
    def _():
        normed[...] = layer_norm(x_ref[...].astype(F32), gain_ref[...]).astype(BF16)

    rows = normed[...]
    for part, (w_ref, b_ref) in enumerate(((wq_ref, bq_ref), (wk_ref, bk_ref), (wv_ref, bv_ref))):
        mixed = (dot(rows, w_ref[...]) + b_ref[...]).astype(BF16).astype(F32)
        if part == 0:
            mixed = mixed * HD_V ** (-0.5)
        turned = mixed.T.astype(BF16)
        for head in range(turned.shape[0] // HD_V):
            piece = turned[head * HD_V : (head + 1) * HD_V]
            for core in range(2):
                out_ref[2 * head + core, part * HD_V : (part + 1) * HD_V, :] = piece


def teacher_mix(patches, gain, weights, bias):
    rows, width = patches.shape
    heads = width // HD_V
    step = 256
    steps = width // step

    def col(part):
        return pl.BlockSpec((width, step), lambda i: (0, part * steps + i))

    def bias_col(part):
        return pl.BlockSpec((1, step), lambda i: (0, part * steps + i))

    return pl.pallas_call(
        teacher_mix_kernel,
        grid=(steps,),
        in_specs=[whole((rows, width)), whole((1, width))]
        + [col(p) for p in range(3)]
        + [bias_col(p) for p in range(3)],
        out_specs=pl.BlockSpec((2 * step // HD_V, 3 * HD_V, rows), lambda i: (i, 0, 0)),
        out_shape=jax.ShapeDtypeStruct((2 * heads, 3 * HD_V, rows), BF16),
        scratch_shapes=[pltpu.VMEM((rows, width), BF16)],
        compiler_params=params(60),
        cost_estimate=cost(rows * width * 3 * width, 8 * MIB),
        name="teacher_mix",
    )(patches, gain, weights, weights, weights, bias, bias, bias)


BOUND = 60.0
TILES = 4


def teacher_attention_kernel(core_ref, mix_ref, out_ref, safe, keys, values, scores):
    tiles, _, rows = mix_ref.shape
    step = pl.program_id(0)
    core = core_ref[0]
    count = tiles * rows

    @pl.when(step == 0)
    def _():
        peaks = [None, None]
        for tile in range(tiles):
            span = slice(tile * rows, (tile + 1) * rows)
            keys[:, span] = mix_ref[tile, HD_V : 2 * HD_V, :]
            turned = mix_ref[tile, 2 * HD_V :, :].astype(F32)
            values[span, :] = jnp.concatenate([turned, jnp.ones_like(turned)], 0).T.astype(BF16)
            for part in range(2):
                piece = mix_ref[tile, part * HD_V : (part + 1) * HD_V, :].astype(F32)
                norms = jnp.sum(piece * piece, 0, keepdims=True)
                peaks[part] = norms if peaks[part] is None else jnp.maximum(peaks[part], norms)
        bound = jnp.max(peaks[0], -1, keepdims=True) * jnp.max(peaks[1], -1, keepdims=True)
        safe[0] = (jnp.max(bound) <= BOUND * BOUND).astype(jnp.int32)

    first = TILES * step
    queries = [mix_ref[2 * (first + i) + core, :HD_V, :].astype(F32) for i in range(TILES)]
    queries = jnp.concatenate(queries, 1).T.astype(BF16)

    def finish(total):
        turned = total.T
        attended = (turned[:HD_V] / turned[HD_V:]).astype(BF16)
        for i in range(TILES):
            out_ref[i] = attended[:, i * rows : (i + 1) * rows]

    @pl.when(safe[0] == 1)
    def _():
        chunk = 512
        total, waiting = None, None
        for start in list(range(0, count, chunk)) + [None]:
            part = None if start is None else dot(queries, keys[:, start : start + chunk])
            if waiting is not None:
                added = dot(waiting[1], values[waiting[0] : waiting[0] + chunk, :])
                total = added if total is None else total + added
            if start is not None:
                waiting = (start, jnp.exp(part).astype(BF16))
        finish(total)

    @pl.when(safe[0] == 0)
    def _():
        chunk = 1024
        top = None
        for start in range(0, count, chunk):
            part = dot(queries, keys[:, start : start + chunk])
            scores[:, start : start + chunk] = part
            peak = jnp.max(part, -1, keepdims=True)
            top = peak if top is None else jnp.maximum(top, peak)
        total = None
        for start in range(0, count, chunk):
            exps = jnp.exp(scores[:, start : start + chunk] - top).astype(BF16)
            part = dot(exps, values[start : start + chunk, :])
            total = part if total is None else total + part
        finish(total)


def teacher_attention(core, mix):
    tiles, depth, rows = mix.shape
    return pl.pallas_call(
        teacher_attention_kernel,
        grid_spec=pltpu.PrefetchScalarGridSpec(
            num_scalar_prefetch=1,
            grid=(tiles // 2 // TILES,),
            in_specs=[whole((tiles, depth, rows))],
            out_specs=pl.BlockSpec((TILES, HD_V, rows), lambda i, c: (i, 0, 0)),
            scratch_shapes=[
                pltpu.SMEM((1,), jnp.int32),
                pltpu.VMEM((HD_V, tiles * rows), BF16),
                pltpu.VMEM((tiles * rows, 128), BF16),
                pltpu.VMEM((TILES * rows, tiles * rows), F32),
            ],
        ),
        out_shape=jax.ShapeDtypeStruct((tiles // 2, HD_V, rows), BF16),
        compiler_params=params(28),
        cost_estimate=cost(2 * tiles * rows * tiles * rows * 128, 2 * MIB, tiles * rows * tiles * rows // 2),
        name="teacher_attention",
    )(core, mix)


def teacher_reply_kernel(me_ref, att_ref, patches_ref, proj_ref, scale_ref, head_ref, asked_ref, out_ref, seen):
    @pl.when(pl.program_id(0) == 0)
    def _():
        heads, depth, rows = att_ref.shape
        attended = att_ref[...].reshape(heads * depth, rows).astype(F32).T.astype(BF16)
        teacher = (patches_ref[...].astype(F32) + scale_ref[...] * dot(attended, proj_ref[...])).astype(BF16)
        through = dot(teacher, head_ref[...], NT)
        wide = teacher.astype(F32)
        seen[...] = (through * lax.rsqrt(jnp.sum(wide * wide, -1, keepdims=True) + eps_norm)).astype(BF16)

    asked = asked_ref[...]
    mine = jnp.sum(jnp.where(lanes(asked.shape) == me_ref[0], asked, 0), -1, keepdims=True)
    hot = jnp.where(lanes((asked.shape[0], seen.shape[0])) == mine - 1, 1.0, 0.0).astype(BF16)
    out_ref[...] = dot(hot, seen[...]).astype(BF16)


def teacher_reply(me, attended, patches, proj, scale, head, asked):
    rows, width = patches.shape
    points = head.shape[0]
    total, devices = asked.shape
    step = total // 6
    return pl.pallas_call(
        teacher_reply_kernel,
        grid_spec=pltpu.PrefetchScalarGridSpec(
            num_scalar_prefetch=1,
            grid=(total // step,),
            in_specs=[
                whole(attended.shape),
                whole((rows, width)),
                whole(proj.shape),
                whole((1, width)),
                whole(head.shape),
                pl.BlockSpec((step, devices), lambda i, m: (i, 0)),
            ],
            out_specs=pl.BlockSpec((step, points), lambda i, m: (i, 0)),
            scratch_shapes=[pltpu.VMEM((rows, points), BF16)],
        ),
        out_shape=jax.ShapeDtypeStruct((total, points), BF16),
        compiler_params=params(60),
        cost_estimate=cost(rows * width * (width + points) + total * rows * points, 9 * MIB),
        name="teacher_reply",
    )(me, attended, patches, proj, scale, head, asked)


def request_kernel(tile_ref, patch_ref, place_ref, asked_ref):
    count = tile_ref.shape[1]
    width = asked_ref.shape[1]
    block = 256
    earlier_than = jnp.where(
        lax.broadcasted_iota(jnp.int32, (block, block), 0) < lanes((block, block)), 1.0, 0.0
    ).astype(BF16)
    before = jnp.zeros((width, 1), F32)
    asked = jnp.zeros((32, width), F32)
    for start in range(0, count, block):
        span = slice(start, start + block)
        tiles = tile_ref[:, span]
        hot = jnp.where(lax.broadcasted_iota(jnp.int32, (width, block), 0) == tiles, 1.0, 0.0)
        earlier = dot(hot.astype(BF16), earlier_than) + before
        before = before + jnp.sum(hot, 1, keepdims=True)
        slot = jnp.sum(earlier * hot, 0, keepdims=True).astype(jnp.int32)
        place_ref[:, span] = tiles * CAP + slot
        slot_hot = jnp.where(lax.broadcasted_iota(jnp.int32, (32, block), 0) == slot, 1.0, 0.0)
        named = (hot * (patch_ref[:, span] + 1).astype(F32)).astype(BF16)
        asked = asked + dot(slot_hot.astype(BF16), named, NT)
    asked_ref[...] = asked[:CAP].astype(jnp.int32)


def requests(tile_ids, patch_ids, devices):
    count = tile_ids.shape[1]
    return pl.pallas_call(
        request_kernel,
        out_shape=(
            jax.ShapeDtypeStruct((1, count), jnp.int32),
            jax.ShapeDtypeStruct((CAP, devices), jnp.int32),
        ),
        compiler_params=params(60),
        cost_estimate=cost(count * 128 * 512, MIB),
        name="requests",
    )(tile_ids, patch_ids)


def point_mix_kernel(order_ref, feats_ref, gain_ref, w_ref, serial_ref, query_ref, pair_ref, peak_ref):
    rows, count = order_ref.shape[1], feats_ref.shape[0]
    hot = jnp.where(lanes((rows, count)) == column(order_ref[...]), 1.0, 0.0).astype(BF16)
    serial = dot(hot, feats_ref[...])
    serial_ref[...] = serial.astype(BF16)
    normed = layer_norm(serial, gain_ref[...]).astype(BF16)
    mixed = dot(normed, w_ref[...]).astype(BF16).astype(F32)
    width = w_ref.shape[1]
    scale = jnp.where(lanes((1, width)) < width // 3, HD_P ** (-0.5), 1.0)
    mixed = mixed * scale
    att = width // 3
    query_ref[...] = mixed[:, :att].astype(BF16)
    for piece in range(2 * att // 128):
        pair_ref[piece] = mixed[:, att + piece * 128 : att + (piece + 1) * 128].astype(BF16)
    head = lax.broadcasted_iota(jnp.int32, (att, att), 0) // HD_P
    head_sum = jnp.where(head == lanes((att, att)) // HD_P, 1.0, 0.0).astype(BF16)
    for part in range(2):
        piece = mixed[:, part * att : (part + 1) * att]
        norms = dot((piece * piece).astype(BF16), head_sum)
        peak = jnp.max(norms, 0, keepdims=True)
        peak_ref[:, part * att : (part + 1) * att] = jnp.broadcast_to(peak, (8, att))


def point_mix(order, feats, gain, weights):
    count, width = feats.shape
    step = MIX_STEP
    att = weights.shape[1] // 3
    return pl.pallas_call(
        point_mix_kernel,
        grid=(count // step,),
        in_specs=[
            pl.BlockSpec((1, step), lambda i: (0, i)),
            whole((count, width)),
            whole((1, width)),
            whole(weights.shape),
        ],
        out_specs=(
            pl.BlockSpec((step, width), lambda i: (i, 0)),
            pl.BlockSpec((step, att), lambda i: (i, 0)),
            pl.BlockSpec((2 * att // 128, step, 128), lambda i: (0, i, 0)),
            pl.BlockSpec((8, 2 * att), lambda i: (i, 0)),
        ),
        out_shape=(
            jax.ShapeDtypeStruct((count, width), BF16),
            jax.ShapeDtypeStruct((count, att), BF16),
            jax.ShapeDtypeStruct((2 * att // 128, count, 128), BF16),
            jax.ShapeDtypeStruct((8 * count // step, 2 * att), F32),
        ),
        compiler_params=params(28),
        cost_estimate=cost(count * width * (count + weights.shape[1]), 9 * MIB),
        name="point_mix",
    )(order, feats, gain, weights)


ROWS = 128
KEYS = 256
GROUP = 128 // HD_P
PARTS = 2


def window_attention_kernel(
    first,
    base_ref,
    count_ref,
    query_ref,
    pair_ref,
    peak_ref,
    window_ref,
    out_ref,
    safe,
    pairs,
    query_mark,
    key_mark,
    stack,
    top,
    total,
):
    points, att = pair_ref.shape[1], query_ref.shape[1]
    groups = att // 128
    stacked = GROUP * ROWS

    @pl.when(pl.program_id(0) == 0)
    def _():
        pairs[...] = pair_ref[...].astype(F32)
        slot = lax.broadcasted_iota(jnp.int32, (128, 128), 0)
        for start in range(0, points, 128):
            window = window_ref[:, start : start + 128]
            other = jnp.where((slot < 4) & (slot != window), -BIG, 0.0)
            key_mark[start : start + 128, :] = other.T
            query_mark[start : start + 128, :] = jnp.where(slot == window, 1.0, 0.0).T.astype(BF16)
        peak = jnp.max(peak_ref[...], 0, keepdims=True)
        safe[0] = (jnp.max(peak[:, :att] * peak[:, att:]) <= BOUND * BOUND).astype(jnp.int32)

    block = pl.program_id(0) + first
    base = base_ref[block]
    steps = count_ref[block]
    here = pl.ds(pl.multiple_of(block * ROWS, ROWS), ROWS)
    lane_head = lanes((ROWS, 128)) // HD_P
    for group in range(groups):
        queries = query_ref[:, group * 128 : (group + 1) * 128]
        for head in range(GROUP):
            span = slice(group * stacked + head * ROWS, group * stacked + (head + 1) * ROWS)
            stack[span, :128] = jnp.where(lane_head == head, queries, jnp.zeros_like(queries))
            stack[span, 128:] = query_mark[here, :]
    def span_of(step, size):
        return pl.ds(base + step * KEYS, size)

    def keys_of(group, span):
        return jnp.concatenate([pairs[group, span, :], key_mark[span, :]], 1).astype(BF16)

    def values_of(group, span):
        values = pairs[groups + group, span, :].astype(BF16)
        return jnp.concatenate([values, jnp.ones_like(values)], 1)

    def fold(step, size):
        span = span_of(step, size)
        rows = stacked // PARTS * 2
        waiting = None

        def add(span, exps, values):
            total[span, :] = jnp.where(step == 0, 0.0, total[span, :]) + dot(exps, values)

        for group in range(groups):
            keys, values = keys_of(group, span), values_of(group, span)
            for start in range(group * stacked, (group + 1) * stacked, rows):
                part = dot(stack[start : start + rows, :], keys, NT)
                if waiting is not None:
                    add(*waiting)
                waiting = (slice(start, start + rows), jnp.exp(part).astype(BF16), values)
        add(*waiting)

    @pl.when(safe[0] == 1)
    def _():
        @pl.loop(0, steps // 4)
        def _(step):
            fold(4 * step, 4 * KEYS)

        @pl.when(steps % 4 >= 2)
        def _():
            fold(steps // 4 * 4, 2 * KEYS)

        @pl.when(steps % 2 == 1)
        def _():
            fold(steps - 1, KEYS)

    @pl.when(safe[0] == 0)
    def _():
        total[...] = jnp.zeros(total.shape, F32)
        for group in range(groups):
            rows = slice(group * stacked, (group + 1) * stacked)
            top[...] = jnp.full(top.shape, -BIG, F32)

            @pl.loop(0, steps)
            def _(step):
                part = dot(stack[rows, :], keys_of(group, span_of(step, KEYS)), NT)
                top[...] = jnp.maximum(top[...], jnp.maximum(part[:, :128], part[:, 128:]))

            top[...] = jnp.broadcast_to(jnp.max(top[...], -1, keepdims=True), top.shape)

            @pl.loop(0, steps)
            def _(step):
                span = span_of(step, KEYS)
                part = dot(stack[rows, :], keys_of(group, span), NT)
                peak = top[...]
                exps = jnp.exp(part - jnp.concatenate([peak, peak], 1)).astype(BF16)
                total[rows, :] += dot(exps, values_of(group, span))

    for group in range(groups):
        over, under = None, None
        for head in range(GROUP):
            span = slice(group * stacked + head * ROWS, group * stacked + (head + 1) * ROWS)
            own = lane_head == head
            over = total[span, :128] if over is None else jnp.where(own, total[span, :128], over)
            under = total[span, 128:] if under is None else jnp.where(own, total[span, 128:], under)
        out_ref[:, group * 128 : (group + 1) * 128] = (over / under).astype(BF16)


def window_ranges(windows):
    points = windows.shape[0]
    blocks = windows.reshape(points // ROWS, ROWS)
    start = jnp.sum((windows[None, :] < blocks[:, :1]).astype(jnp.int32), 1)
    end = jnp.sum((windows[None, :] <= blocks[:, -1:]).astype(jnp.int32), 1)
    count = (end - start + KEYS - 1) // KEYS
    base = jnp.minimum(start, points - count * KEYS)
    return base, count


def window_attention(queries, pairs, peaks, window_row, base, count, first, blocks):
    points, att = queries.shape
    stacked = GROUP * ROWS
    return pl.pallas_call(
        functools.partial(window_attention_kernel, first),
        grid_spec=pltpu.PrefetchScalarGridSpec(
            num_scalar_prefetch=2,
            grid=(blocks,),
            in_specs=[pl.BlockSpec((ROWS, att), lambda i, b, c: (i + first, 0)), whole(pairs.shape), whole(peaks.shape), whole((1, points))],
            out_specs=pl.BlockSpec((ROWS, att), lambda i, b, c: (i, 0)),
            scratch_shapes=[
                pltpu.SMEM((1,), jnp.int32),
                pltpu.VMEM(pairs.shape, F32),
                pltpu.VMEM((points, 128), BF16),
                pltpu.VMEM((points, 128), F32),
                pltpu.VMEM((att // 128 * stacked, 256), BF16),
                pltpu.VMEM((stacked, 128), F32),
                pltpu.VMEM((att // 128 * stacked, 256), F32),
            ],
        ),
        out_shape=jax.ShapeDtypeStruct((blocks * ROWS, att), BF16),
        compiler_params=params(40),
        cost_estimate=cost(
            blocks * ROWS * 1024 * 16 * 512, 5 * MIB, blocks * ROWS * 1024 * 16
        ),
        name="window_attention",
    )(base, count, queries, pairs, peaks, window_row)


def point_block_kernel(serial_ref, att_ref, proj_ref, gain_ref, up_ref, down_ref, head_ref, out_ref, norm_ref):
    residual = serial_ref[...].astype(F32) + dot(att_ref[...], proj_ref[...])
    normed = layer_norm(residual, gain_ref[...]).astype(BF16)
    hidden_width = up_ref.shape[1]
    chunk = HIDDEN
    added = None
    for start in range(0, hidden_width, chunk):
        before = dot(normed, up_ref[:, start : start + chunk])
        hidden = (0.5 * before * (1.0 + lax.erf(before * (0.5**0.5)))).astype(BF16)
        part = dot(hidden, down_ref[start : start + chunk, :])
        added = part if added is None else added + part
    block_out = (residual + added).astype(BF16)
    out_ref[...] = block_out
    student = dot(block_out, head_ref[...])
    norm_ref[...] = jnp.sum(student * student, -1, keepdims=True)


def point_block(serial, attended, proj, gain, up, down, head):
    count, width = serial.shape
    att = attended.shape[1]
    step = BLOCK_STEP
    return pl.pallas_call(
        point_block_kernel,
        grid=(count // step,),
        in_specs=[
            pl.BlockSpec((step, width), lambda i: (i, 0)),
            pl.BlockSpec((step, att), lambda i: (i, 0)),
            whole(proj.shape),
            whole((1, width)),
            whole(up.shape),
            whole(down.shape),
            whole(head.shape),
        ],
        out_specs=(
            pl.BlockSpec((step, width), lambda i: (i, 0)),
            pl.BlockSpec((step, 1), lambda i: (i, 0)),
        ),
        out_shape=(
            jax.ShapeDtypeStruct((count, width), BF16),
            jax.ShapeDtypeStruct((count, 1), F32),
        ),
        compiler_params=params(36),
        cost_estimate=cost(
            count * width * (att + 2 * up.shape[1] + head.shape[1]), 12 * MIB, count * up.shape[1]
        ),
        name="point_block",
    )(serial, attended, proj, gain, up, down, head)


def loss_kernel(place_ref, out_ref, norm_ref, replies_ref, loss_ref):
    rows, total = place_ref.shape[1], replies_ref.shape[0]
    hot = jnp.where(lanes((rows, total)) == column(place_ref[...]), 1.0, 0.0).astype(BF16)
    target = dot(hot, replies_ref[...])
    inner = jnp.sum(out_ref[...].astype(F32) * target, -1, keepdims=True)
    loss_ref[...] = 1.0 - row_of(inner * lax.rsqrt(norm_ref[...] + eps_norm))


def loss(place, point_out, norms, replies):
    count, width = point_out.shape
    step = LOSS_STEP
    return pl.pallas_call(
        loss_kernel,
        grid=(count // step,),
        in_specs=[
            pl.BlockSpec((1, step), lambda i: (0, i)),
            pl.BlockSpec((step, width), lambda i: (i, 0)),
            pl.BlockSpec((step, 1), lambda i: (i, 0)),
            whole(replies.shape),
        ],
        out_specs=pl.BlockSpec((1, step), lambda i: (0, i)),
        out_shape=jax.ShapeDtypeStruct((1, count), F32),
        compiler_params=params(40),
        cost_estimate=cost(count * width * replies.shape[0], 8 * MIB),
        name="loss",
    )(place, point_out, norms, replies)


def local(
    patches,
    vit_gain,
    vit_qkv,
    vit_qkv_bias,
    vit_proj,
    vit_scale,
    point_feats,
    point_order,
    window_ids,
    point_tile,
    point_patch,
    pt_gain,
    pt_qkv,
    pt_proj,
    pt_up,
    pt_down,
    head_w,
):
    both = ("cam", "tile")
    tile_count = lax.axis_size("tile")
    device_count = lax.axis_size("cam") * tile_count
    tile_index = lax.axis_index("tile")
    me = (lax.axis_index("cam") * tile_count + tile_index).astype(jnp.int32).reshape(1)
    core = (tile_index % 2).astype(jnp.int32).reshape(1)
    count = point_feats.shape[0]

    mix = teacher_mix(patches[0], vit_gain[None], vit_qkv, vit_qkv_bias[None])
    mix = lax.all_to_all(mix, "tile", split_axis=0, concat_axis=0, tiled=True)

    place, asked = requests(point_tile.reshape(1, count), point_patch.reshape(1, count), device_count)
    asked = lax.all_gather(asked, both, axis=0, tiled=True)
    serial, queries, pairs, peaks = point_mix(
        point_order, point_feats, pt_gain[:1], pt_qkv
    )
    base, steps = window_ranges(window_ids[0])
    blocks = count // ROWS
    cuts = (0, blocks // 8, 5 * blocks // 16, blocks)

    def attend(part, base):
        return window_attention(
            queries, pairs, peaks, window_ids, base, steps, cuts[part], cuts[part + 1] - cuts[part]
        )

    parts = [attend(0, base)]
    mix, parts[0] = lax.optimization_barrier((mix, parts[0]))
    attended = teacher_attention(core, mix)
    groups = [[2 * i + c for i in range(tile_count // 2)] for c in range(2)]
    attended, base = lax.optimization_barrier((attended, base))
    attended = lax.all_to_all(
        attended, "tile", split_axis=0, concat_axis=0, tiled=True, axis_index_groups=groups
    )
    parts.append(attend(1, base))
    attended, parts[1], base = lax.optimization_barrier((attended, parts[1], base))
    replies = teacher_reply(me, attended, patches[0], vit_proj, vit_scale[None], head_w, asked)
    replies, base = lax.optimization_barrier((replies, base))
    replies = lax.all_to_all(
        replies.reshape(device_count, CAP, -1), both, split_axis=0, concat_axis=0, tiled=True
    ).reshape(device_count * CAP, -1)
    parts.append(attend(2, base))
    pt_attended = jnp.concatenate(parts, 0)
    point_out, norms = point_block(serial, pt_attended, pt_proj, pt_gain[1:], pt_up, pt_down, head_w)
    losses = loss(place, point_out, norms, replies)
    return (point_out, losses.reshape(count))


def solution(mesh):
    both = ("cam", "tile")
    placed = (
        P("cam", "tile", None),
        P(),
        P(),
        P(),
        P(),
        P(),
        P(both, None),
        P(both, None),
        P(both, None),
        P(both, None),
        P(both),
        P(),
        P(),
        P(),
        P(),
        P(),
        P(),
    )
    return jax.shard_map(
        local,
        mesh=mesh,
        in_specs=placed,
        out_specs=(P(both, None), P(both)),
        check_vma=False,
    )
```

```python
import functools

import jax
import jax.numpy as jnp
from jax import lax
from jax.experimental import pallas as pl
from jax.experimental.pallas import tpu as pltpu
from jax.sharding import PartitionSpec as P

HD_V = 64
HD_P = 16
CAP = 24
eps_norm = 1e-06
BIG = 1e30
MIB = 1024 * 1024
F32 = jnp.float32
BF16 = jnp.bfloat16
NT = (((1,), (1,)), ((), ()))
TN = (((0,), (0,)), ((), ()))
MIX_STEP = 512
BLOCK_STEP = 512
HIDDEN = 512
LOSS_STEP = 512


def layer_norm(values, gain):
    center = values - jnp.mean(values, -1, keepdims=True)
    spread = jnp.mean(center * center, -1, keepdims=True)
    return center * lax.rsqrt(spread + eps_norm) * gain


def dot(left, right, dims=None):
    if dims is None:
        return jnp.dot(left, right, preferred_element_type=F32)
    return lax.dot_general(left, right, dims, preferred_element_type=F32)


def lanes(shape):
    return lax.broadcasted_iota(jnp.int32, shape, len(shape) - 1)


def column(row):
    pieces = []
    for start in range(0, row.shape[1], 128):
        own = lanes((128, 128)) == lax.broadcasted_iota(jnp.int32, (128, 128), 0)
        pieces.append(jnp.sum(jnp.where(own, row[:, start : start + 128], 0), 1, keepdims=True))
    return jnp.concatenate(pieces, 0)


def row_of(col):
    pieces = []
    for start in range(0, col.shape[0], 128):
        own = lanes((128, 128)) == lax.broadcasted_iota(jnp.int32, (128, 128), 0)
        pieces.append(jnp.sum(jnp.where(own, col[start : start + 128], 0), 0, keepdims=True))
    return jnp.concatenate(pieces, 1)


def whole(shape):
    return pl.BlockSpec(shape, lambda *_: (0,) * len(shape))


def params(limit):
    return pltpu.CompilerParams(vmem_limit_bytes=limit * MIB)


def cost(macs, moved, exps=0):
    return pl.CostEstimate(flops=2 * macs, bytes_accessed=moved, transcendentals=exps)


def teacher_mix_kernel(x_ref, gain_ref, wq_ref, wk_ref, wv_ref, bq_ref, bk_ref, bv_ref, out_ref, normed):
    @pl.when(pl.program_id(0) == 0)
    def _():
        normed[...] = layer_norm(x_ref[...].astype(F32), gain_ref[...]).astype(BF16)

    rows = normed[...]
    for part, (w_ref, b_ref) in enumerate(((wq_ref, bq_ref), (wk_ref, bk_ref), (wv_ref, bv_ref))):
        mixed = (dot(rows, w_ref[...]) + b_ref[...]).astype(BF16).astype(F32)
        if part == 0:
            mixed = mixed * HD_V ** (-0.5)
        turned = mixed.T.astype(BF16)
        for head in range(turned.shape[0] // HD_V):
            piece = turned[head * HD_V : (head + 1) * HD_V]
            for core in range(2):
                out_ref[2 * head + core, part * HD_V : (part + 1) * HD_V, :] = piece


def teacher_mix(patches, gain, weights, bias):
    rows, width = patches.shape
    heads = width // HD_V
    step = 256
    steps = width // step

    def col(part):
        return pl.BlockSpec((width, step), lambda i: (0, part * steps + i))

    def bias_col(part):
        return pl.BlockSpec((1, step), lambda i: (0, part * steps + i))

    return pl.pallas_call(
        teacher_mix_kernel,
        grid=(steps,),
        in_specs=[whole((rows, width)), whole((1, width))]
        + [col(p) for p in range(3)]
        + [bias_col(p) for p in range(3)],
        out_specs=pl.BlockSpec((2 * step // HD_V, 3 * HD_V, rows), lambda i: (i, 0, 0)),
        out_shape=jax.ShapeDtypeStruct((2 * heads, 3 * HD_V, rows), BF16),
        scratch_shapes=[pltpu.VMEM((rows, width), BF16)],
        compiler_params=params(60),
        cost_estimate=cost(rows * width * 3 * width, 8 * MIB),
        name="teacher_mix",
    )(patches, gain, weights, weights, weights, bias, bias, bias)


BOUND = 60.0
TILES = 4


def teacher_attention_kernel(core_ref, mix_ref, out_ref, safe, keys, values, scores):
    tiles, _, rows = mix_ref.shape
    step = pl.program_id(0)
    core = core_ref[0]
    count = tiles * rows

    @pl.when(step == 0)
    def _():
        peaks = [None, None]
        for tile in range(tiles):
            span = slice(tile * rows, (tile + 1) * rows)
            keys[:, span] = mix_ref[tile, HD_V : 2 * HD_V, :]
            turned = mix_ref[tile, 2 * HD_V :, :].astype(F32)
            values[span, :] = jnp.concatenate([turned, jnp.ones_like(turned)], 0).T.astype(BF16)
            for part in range(2):
                piece = mix_ref[tile, part * HD_V : (part + 1) * HD_V, :].astype(F32)
                norms = jnp.sum(piece * piece, 0, keepdims=True)
                peaks[part] = norms if peaks[part] is None else jnp.maximum(peaks[part], norms)
        bound = jnp.max(peaks[0], -1, keepdims=True) * jnp.max(peaks[1], -1, keepdims=True)
        safe[0] = (jnp.max(bound) <= BOUND * BOUND).astype(jnp.int32)

    first = TILES * step
    queries = [mix_ref[2 * (first + i) + core, :HD_V, :].astype(F32) for i in range(TILES)]
    queries = jnp.concatenate(queries, 1).T.astype(BF16)

    def finish(total):
        turned = total.T
        attended = (turned[:HD_V] / turned[HD_V:]).astype(BF16)
        for i in range(TILES):
            out_ref[i] = attended[:, i * rows : (i + 1) * rows]

    @pl.when(safe[0] == 1)
    def _():
        chunk = 512
        total, waiting = None, None
        for start in list(range(0, count, chunk)) + [None]:
            part = None if start is None else dot(queries, keys[:, start : start + chunk])
            if waiting is not None:
                added = dot(waiting[1], values[waiting[0] : waiting[0] + chunk, :])
                total = added if total is None else total + added
            if start is not None:
                waiting = (start, jnp.exp(part).astype(BF16))
        finish(total)

    @pl.when(safe[0] == 0)
    def _():
        chunk = 1024
        top = None
        for start in range(0, count, chunk):
            part = dot(queries, keys[:, start : start + chunk])
            scores[:, start : start + chunk] = part
            peak = jnp.max(part, -1, keepdims=True)
            top = peak if top is None else jnp.maximum(top, peak)
        total = None
        for start in range(0, count, chunk):
            exps = jnp.exp(scores[:, start : start + chunk] - top).astype(BF16)
            part = dot(exps, values[start : start + chunk, :])
            total = part if total is None else total + part
        finish(total)


def teacher_attention(core, mix):
    tiles, depth, rows = mix.shape
    return pl.pallas_call(
        teacher_attention_kernel,
        grid_spec=pltpu.PrefetchScalarGridSpec(
            num_scalar_prefetch=1,
            grid=(tiles // 2 // TILES,),
            in_specs=[whole((tiles, depth, rows))],
            out_specs=pl.BlockSpec((TILES, HD_V, rows), lambda i, c: (i, 0, 0)),
            scratch_shapes=[
                pltpu.SMEM((1,), jnp.int32),
                pltpu.VMEM((HD_V, tiles * rows), BF16),
                pltpu.VMEM((tiles * rows, 128), BF16),
                pltpu.VMEM((TILES * rows, tiles * rows), F32),
            ],
        ),
        out_shape=jax.ShapeDtypeStruct((tiles // 2, HD_V, rows), BF16),
        compiler_params=params(28),
        cost_estimate=cost(2 * tiles * rows * tiles * rows * 128, 2 * MIB, tiles * rows * tiles * rows // 2),
        name="teacher_attention",
    )(core, mix)


def teacher_reply_kernel(me_ref, att_ref, patches_ref, proj_ref, scale_ref, head_ref, asked_ref, out_ref, seen):
    @pl.when(pl.program_id(0) == 0)
    def _():
        heads, depth, rows = att_ref.shape
        attended = att_ref[...].reshape(heads * depth, rows).astype(F32).T.astype(BF16)
        teacher = (patches_ref[...].astype(F32) + scale_ref[...] * dot(attended, proj_ref[...])).astype(BF16)
        through = dot(teacher, head_ref[...], NT)
        wide = teacher.astype(F32)
        seen[...] = (through * lax.rsqrt(jnp.sum(wide * wide, -1, keepdims=True) + eps_norm)).astype(BF16)

    asked = asked_ref[...]
    mine = jnp.sum(jnp.where(lanes(asked.shape) == me_ref[0], asked, 0), -1, keepdims=True)
    hot = jnp.where(lanes((asked.shape[0], seen.shape[0])) == mine - 1, 1.0, 0.0).astype(BF16)
    out_ref[...] = dot(hot, seen[...]).astype(BF16)


def teacher_reply(me, attended, patches, proj, scale, head, asked):
    rows, width = patches.shape
    points = head.shape[0]
    total, devices = asked.shape
    step = total // 6
    return pl.pallas_call(
        teacher_reply_kernel,
        grid_spec=pltpu.PrefetchScalarGridSpec(
            num_scalar_prefetch=1,
            grid=(total // step,),
            in_specs=[
                whole(attended.shape),
                whole((rows, width)),
                whole(proj.shape),
                whole((1, width)),
                whole(head.shape),
                pl.BlockSpec((step, devices), lambda i, m: (i, 0)),
            ],
            out_specs=pl.BlockSpec((step, points), lambda i, m: (i, 0)),
            scratch_shapes=[pltpu.VMEM((rows, points), BF16)],
        ),
        out_shape=jax.ShapeDtypeStruct((total, points), BF16),
        compiler_params=params(60),
        cost_estimate=cost(rows * width * (width + points) + total * rows * points, 9 * MIB),
        name="teacher_reply",
    )(me, attended, patches, proj, scale, head, asked)


def request_kernel(tile_ref, patch_ref, place_ref, asked_ref):
    count = tile_ref.shape[1]
    width = asked_ref.shape[1]
    block = 256
    earlier_than = jnp.where(
        lax.broadcasted_iota(jnp.int32, (block, block), 0) < lanes((block, block)), 1.0, 0.0
    ).astype(BF16)
    before = jnp.zeros((width, 1), F32)
    asked = jnp.zeros((32, width), F32)
    for start in range(0, count, block):
        span = slice(start, start + block)
        tiles = tile_ref[:, span]
        hot = jnp.where(lax.broadcasted_iota(jnp.int32, (width, block), 0) == tiles, 1.0, 0.0)
        earlier = dot(hot.astype(BF16), earlier_than) + before
        before = before + jnp.sum(hot, 1, keepdims=True)
        slot = jnp.sum(earlier * hot, 0, keepdims=True).astype(jnp.int32)
        place_ref[:, span] = tiles * CAP + slot
        slot_hot = jnp.where(lax.broadcasted_iota(jnp.int32, (32, block), 0) == slot, 1.0, 0.0)
        named = (hot * (patch_ref[:, span] + 1).astype(F32)).astype(BF16)
        asked = asked + dot(slot_hot.astype(BF16), named, NT)
    asked_ref[...] = asked[:CAP].astype(jnp.int32)


def requests(tile_ids, patch_ids, devices):
    count = tile_ids.shape[1]
    return pl.pallas_call(
        request_kernel,
        out_shape=(
            jax.ShapeDtypeStruct((1, count), jnp.int32),
            jax.ShapeDtypeStruct((CAP, devices), jnp.int32),
        ),
        compiler_params=params(60),
        cost_estimate=cost(count * 128 * 512, MIB),
        name="requests",
    )(tile_ids, patch_ids)


def point_mix_kernel(order_ref, feats_ref, gain_ref, w_ref, serial_ref, query_ref, pair_ref, peak_ref):
    rows, count = order_ref.shape[1], feats_ref.shape[0]
    hot = jnp.where(lanes((rows, count)) == column(order_ref[...]), 1.0, 0.0).astype(BF16)
    serial = dot(hot, feats_ref[...])
    serial_ref[...] = serial.astype(BF16)
    normed = layer_norm(serial, gain_ref[...]).astype(BF16)
    mixed = dot(normed, w_ref[...]).astype(BF16).astype(F32)
    width = w_ref.shape[1]
    scale = jnp.where(lanes((1, width)) < width // 3, HD_P ** (-0.5), 1.0)
    mixed = mixed * scale
    att = width // 3
    query_ref[...] = mixed[:, :att].astype(BF16)
    for piece in range(2 * att // 128):
        pair_ref[piece] = mixed[:, att + piece * 128 : att + (piece + 1) * 128].astype(BF16)
    head = lax.broadcasted_iota(jnp.int32, (att, att), 0) // HD_P
    head_sum = jnp.where(head == lanes((att, att)) // HD_P, 1.0, 0.0).astype(BF16)
    for part in range(2):
        piece = mixed[:, part * att : (part + 1) * att]
        norms = dot((piece * piece).astype(BF16), head_sum)
        peak = jnp.max(norms, 0, keepdims=True)
        peak_ref[:, part * att : (part + 1) * att] = jnp.broadcast_to(peak, (8, att))


def point_mix(order, feats, gain, weights):
    count, width = feats.shape
    step = MIX_STEP
    att = weights.shape[1] // 3
    return pl.pallas_call(
        point_mix_kernel,
        grid=(count // step,),
        in_specs=[
            pl.BlockSpec((1, step), lambda i: (0, i)),
            whole((count, width)),
            whole((1, width)),
            whole(weights.shape),
        ],
        out_specs=(
            pl.BlockSpec((step, width), lambda i: (i, 0)),
            pl.BlockSpec((step, att), lambda i: (i, 0)),
            pl.BlockSpec((2 * att // 128, step, 128), lambda i: (0, i, 0)),
            pl.BlockSpec((8, 2 * att), lambda i: (i, 0)),
        ),
        out_shape=(
            jax.ShapeDtypeStruct((count, width), BF16),
            jax.ShapeDtypeStruct((count, att), BF16),
            jax.ShapeDtypeStruct((2 * att // 128, count, 128), BF16),
            jax.ShapeDtypeStruct((8 * count // step, 2 * att), F32),
        ),
        compiler_params=params(28),
        cost_estimate=cost(count * width * (count + weights.shape[1]), 9 * MIB),
        name="point_mix",
    )(order, feats, gain, weights)


ROWS = 128
KEYS = 256
GROUP = 128 // HD_P
PARTS = 2


def window_attention_kernel(
    first,
    base_ref,
    count_ref,
    query_ref,
    pair_ref,
    peak_ref,
    window_ref,
    out_ref,
    safe,
    pairs,
    query_mark,
    key_mark,
    stack,
    top,
    total,
):
    points, att = pair_ref.shape[1], query_ref.shape[1]
    groups = att // 128
    stacked = GROUP * ROWS

    @pl.when(pl.program_id(0) == 0)
    def _():
        pairs[...] = pair_ref[...].astype(F32)
        slot = lax.broadcasted_iota(jnp.int32, (128, 128), 0)
        for start in range(0, points, 128):
            window = window_ref[:, start : start + 128]
            other = jnp.where((slot < 4) & (slot != window), -BIG, 0.0)
            key_mark[start : start + 128, :] = other.T
            query_mark[start : start + 128, :] = jnp.where(slot == window, 1.0, 0.0).T.astype(BF16)
        peak = jnp.max(peak_ref[...], 0, keepdims=True)
        safe[0] = (jnp.max(peak[:, :att] * peak[:, att:]) <= BOUND * BOUND).astype(jnp.int32)

    block = pl.program_id(0) + first
    base = base_ref[block]
    steps = count_ref[block]
    here = pl.ds(pl.multiple_of(block * ROWS, ROWS), ROWS)
    lane_head = lanes((ROWS, 128)) // HD_P
    for group in range(groups):
        queries = query_ref[:, group * 128 : (group + 1) * 128]
        for head in range(GROUP):
            span = slice(group * stacked + head * ROWS, group * stacked + (head + 1) * ROWS)
            stack[span, :128] = jnp.where(lane_head == head, queries, jnp.zeros_like(queries))
            stack[span, 128:] = query_mark[here, :]
    def span_of(step, size):
        return pl.ds(base + step * KEYS, size)

    def keys_of(group, span):
        return jnp.concatenate([pairs[group, span, :], key_mark[span, :]], 1).astype(BF16)

    def values_of(group, span):
        values = pairs[groups + group, span, :].astype(BF16)
        return jnp.concatenate([values, jnp.ones_like(values)], 1)

    def fold(step, size):
        span = span_of(step, size)
        rows = stacked // PARTS * 2
        waiting = None

        def add(span, exps, values):
            total[span, :] = jnp.where(step == 0, 0.0, total[span, :]) + dot(exps, values)

        for group in range(groups):
            keys, values = keys_of(group, span), values_of(group, span)
            for start in range(group * stacked, (group + 1) * stacked, rows):
                part = dot(stack[start : start + rows, :], keys, NT)
                if waiting is not None:
                    add(*waiting)
                waiting = (slice(start, start + rows), jnp.exp(part).astype(BF16), values)
        add(*waiting)

    @pl.when(safe[0] == 1)
    def _():
        @pl.loop(0, steps // 4)
        def _(step):
            fold(4 * step, 4 * KEYS)

        @pl.when(steps % 4 >= 2)
        def _():
            fold(steps // 4 * 4, 2 * KEYS)

        @pl.when(steps % 2 == 1)
        def _():
            fold(steps - 1, KEYS)

    @pl.when(safe[0] == 0)
    def _():
        total[...] = jnp.zeros(total.shape, F32)
        for group in range(groups):
            rows = slice(group * stacked, (group + 1) * stacked)
            top[...] = jnp.full(top.shape, -BIG, F32)

            @pl.loop(0, steps)
            def _(step):
                part = dot(stack[rows, :], keys_of(group, span_of(step, KEYS)), NT)
                top[...] = jnp.maximum(top[...], jnp.maximum(part[:, :128], part[:, 128:]))

            top[...] = jnp.broadcast_to(jnp.max(top[...], -1, keepdims=True), top.shape)

            @pl.loop(0, steps)
            def _(step):
                span = span_of(step, KEYS)
                part = dot(stack[rows, :], keys_of(group, span), NT)
                peak = top[...]
                exps = jnp.exp(part - jnp.concatenate([peak, peak], 1)).astype(BF16)
                total[rows, :] += dot(exps, values_of(group, span))

    for group in range(groups):
        over, under = None, None
        for head in range(GROUP):
            span = slice(group * stacked + head * ROWS, group * stacked + (head + 1) * ROWS)
            own = lane_head == head
            over = total[span, :128] if over is None else jnp.where(own, total[span, :128], over)
            under = total[span, 128:] if under is None else jnp.where(own, total[span, 128:], under)
        out_ref[:, group * 128 : (group + 1) * 128] = (over / under).astype(BF16)


def window_ranges(windows):
    points = windows.shape[0]
    blocks = windows.reshape(points // ROWS, ROWS)
    start = jnp.sum((windows[None, :] < blocks[:, :1]).astype(jnp.int32), 1)
    end = jnp.sum((windows[None, :] <= blocks[:, -1:]).astype(jnp.int32), 1)
    count = (end - start + KEYS - 1) // KEYS
    base = jnp.minimum(start, points - count * KEYS)
    return base, count


def window_attention(queries, pairs, peaks, window_row, base, count, first, blocks):
    points, att = queries.shape
    stacked = GROUP * ROWS
    return pl.pallas_call(
        functools.partial(window_attention_kernel, first),
        grid_spec=pltpu.PrefetchScalarGridSpec(
            num_scalar_prefetch=2,
            grid=(blocks,),
            in_specs=[pl.BlockSpec((ROWS, att), lambda i, b, c: (i + first, 0)), whole(pairs.shape), whole(peaks.shape), whole((1, points))],
            out_specs=pl.BlockSpec((ROWS, att), lambda i, b, c: (i, 0)),
            scratch_shapes=[
                pltpu.SMEM((1,), jnp.int32),
                pltpu.VMEM(pairs.shape, F32),
                pltpu.VMEM((points, 128), BF16),
                pltpu.VMEM((points, 128), F32),
                pltpu.VMEM((att // 128 * stacked, 256), BF16),
                pltpu.VMEM((stacked, 128), F32),
                pltpu.VMEM((att // 128 * stacked, 256), F32),
            ],
        ),
        out_shape=jax.ShapeDtypeStruct((blocks * ROWS, att), BF16),
        compiler_params=params(40),
        cost_estimate=cost(
            blocks * ROWS * 1024 * 16 * 512, 5 * MIB, blocks * ROWS * 1024 * 16
        ),
        name="window_attention",
    )(base, count, queries, pairs, peaks, window_row)


def point_block_kernel(serial_ref, att_ref, proj_ref, gain_ref, up_ref, down_ref, head_ref, out_ref, norm_ref):
    residual = serial_ref[...].astype(F32) + dot(att_ref[...], proj_ref[...])
    normed = layer_norm(residual, gain_ref[...]).astype(BF16)
    hidden_width = up_ref.shape[1]
    chunk = HIDDEN
    added = None
    for start in range(0, hidden_width, chunk):
        before = dot(normed, up_ref[:, start : start + chunk])
        hidden = (0.5 * before * (1.0 + lax.erf(before * (0.5**0.5)))).astype(BF16)
        part = dot(hidden, down_ref[start : start + chunk, :])
        added = part if added is None else added + part
    block_out = (residual + added).astype(BF16)
    out_ref[...] = block_out
    student = dot(block_out, head_ref[...])
    norm_ref[...] = jnp.sum(student * student, -1, keepdims=True)


def point_block(serial, attended, proj, gain, up, down, head):
    count, width = serial.shape
    att = attended.shape[1]
    step = BLOCK_STEP
    return pl.pallas_call(
        point_block_kernel,
        grid=(count // step,),
        in_specs=[
            pl.BlockSpec((step, width), lambda i: (i, 0)),
            pl.BlockSpec((step, att), lambda i: (i, 0)),
            whole(proj.shape),
            whole((1, width)),
            whole(up.shape),
            whole(down.shape),
            whole(head.shape),
        ],
        out_specs=(
            pl.BlockSpec((step, width), lambda i: (i, 0)),
            pl.BlockSpec((step, 1), lambda i: (i, 0)),
        ),
        out_shape=(
            jax.ShapeDtypeStruct((count, width), BF16),
            jax.ShapeDtypeStruct((count, 1), F32),
        ),
        compiler_params=params(36),
        cost_estimate=cost(
            count * width * (att + 2 * up.shape[1] + head.shape[1]), 12 * MIB, count * up.shape[1]
        ),
        name="point_block",
    )(serial, attended, proj, gain, up, down, head)


def loss_kernel(place_ref, out_ref, norm_ref, replies_ref, loss_ref):
    rows, total = place_ref.shape[1], replies_ref.shape[0]
    hot = jnp.where(lanes((rows, total)) == column(place_ref[...]), 1.0, 0.0).astype(BF16)
    target = dot(hot, replies_ref[...])
    inner = jnp.sum(out_ref[...].astype(F32) * target, -1, keepdims=True)
    loss_ref[...] = 1.0 - row_of(inner * lax.rsqrt(norm_ref[...] + eps_norm))


def loss(place, point_out, norms, replies):
    count, width = point_out.shape
    step = LOSS_STEP
    return pl.pallas_call(
        loss_kernel,
        grid=(count // step,),
        in_specs=[
            pl.BlockSpec((1, step), lambda i: (0, i)),
            pl.BlockSpec((step, width), lambda i: (i, 0)),
            pl.BlockSpec((step, 1), lambda i: (i, 0)),
            whole(replies.shape),
        ],
        out_specs=pl.BlockSpec((1, step), lambda i: (0, i)),
        out_shape=jax.ShapeDtypeStruct((1, count), F32),
        compiler_params=params(40),
        cost_estimate=cost(count * width * replies.shape[0], 8 * MIB),
        name="loss",
    )(place, point_out, norms, replies)


def local(
    patches,
    vit_gain,
    vit_qkv,
    vit_qkv_bias,
    vit_proj,
    vit_scale,
    point_feats,
    point_order,
    window_ids,
    point_tile,
    point_patch,
    pt_gain,
    pt_qkv,
    pt_proj,
    pt_up,
    pt_down,
    head_w,
):
    both = ("cam", "tile")
    tile_count = lax.axis_size("tile")
    device_count = lax.axis_size("cam") * tile_count
    tile_index = lax.axis_index("tile")
    me = (lax.axis_index("cam") * tile_count + tile_index).astype(jnp.int32).reshape(1)
    core = (tile_index % 2).astype(jnp.int32).reshape(1)
    count = point_feats.shape[0]

    mix = teacher_mix(patches[0], vit_gain[None], vit_qkv, vit_qkv_bias[None])
    mix = lax.all_to_all(mix, "tile", split_axis=0, concat_axis=0, tiled=True)

    place, asked = requests(point_tile.reshape(1, count), point_patch.reshape(1, count), device_count)
    asked = lax.all_gather(asked, both, axis=0, tiled=True)
    serial, queries, pairs, peaks = point_mix(
        point_order, point_feats, pt_gain[:1], pt_qkv
    )
    base, steps = window_ranges(window_ids[0])
    blocks = count // ROWS
    cuts = (0, blocks // 8, 7 * blocks // 16, blocks)

    def attend(part, base):
        return window_attention(
            queries, pairs, peaks, window_ids, base, steps, cuts[part], cuts[part + 1] - cuts[part]
        )

    parts = [attend(0, base)]
    mix, parts[0] = lax.optimization_barrier((mix, parts[0]))
    attended = teacher_attention(core, mix)
    groups = [[2 * i + c for i in range(tile_count // 2)] for c in range(2)]
    attended, base = lax.optimization_barrier((attended, base))
    attended = lax.all_to_all(
        attended, "tile", split_axis=0, concat_axis=0, tiled=True, axis_index_groups=groups
    )
    parts.append(attend(1, base))
    attended, parts[1], base = lax.optimization_barrier((attended, parts[1], base))
    replies = teacher_reply(me, attended, patches[0], vit_proj, vit_scale[None], head_w, asked)
    replies, base = lax.optimization_barrier((replies, base))
    replies = lax.all_to_all(
        replies.reshape(device_count, CAP, -1), both, split_axis=0, concat_axis=0, tiled=True
    ).reshape(device_count * CAP, -1)
    parts.append(attend(2, base))
    pt_attended = jnp.concatenate(parts, 0)
    point_out, norms = point_block(serial, pt_attended, pt_proj, pt_gain[1:], pt_up, pt_down, head_w)
    losses = loss(place, point_out, norms, replies)
    return (point_out, losses.reshape(count))


def solution(mesh):
    both = ("cam", "tile")
    placed = (
        P("cam", "tile", None),
        P(),
        P(),
        P(),
        P(),
        P(),
        P(both, None),
        P(both, None),
        P(both, None),
        P(both, None),
        P(both),
        P(),
        P(),
        P(),
        P(),
        P(),
        P(),
    )
    return jax.shard_map(
        local,
        mesh=mesh,
        in_specs=placed,
        out_specs=(P(both, None), P(both)),
        check_vma=False,
    )
```

```python
import functools

import jax
import jax.numpy as jnp
from jax import lax
from jax.experimental import pallas as pl
from jax.experimental.pallas import tpu as pltpu
from jax.sharding import PartitionSpec as P

HD_V = 64
HD_P = 16
CAP = 24
eps_norm = 1e-06
BIG = 1e30
MIB = 1024 * 1024
F32 = jnp.float32
BF16 = jnp.bfloat16
NT = (((1,), (1,)), ((), ()))
TN = (((0,), (0,)), ((), ()))
MIX_STEP = 512
BLOCK_STEP = 512
HIDDEN = 512
LOSS_STEP = 512


def layer_norm(values, gain):
    center = values - jnp.mean(values, -1, keepdims=True)
    spread = jnp.mean(center * center, -1, keepdims=True)
    return center * lax.rsqrt(spread + eps_norm) * gain


def dot(left, right, dims=None):
    if dims is None:
        return jnp.dot(left, right, preferred_element_type=F32)
    return lax.dot_general(left, right, dims, preferred_element_type=F32)


def lanes(shape):
    return lax.broadcasted_iota(jnp.int32, shape, len(shape) - 1)


def column(row):
    pieces = []
    for start in range(0, row.shape[1], 128):
        own = lanes((128, 128)) == lax.broadcasted_iota(jnp.int32, (128, 128), 0)
        pieces.append(jnp.sum(jnp.where(own, row[:, start : start + 128], 0), 1, keepdims=True))
    return jnp.concatenate(pieces, 0)


def row_of(col):
    pieces = []
    for start in range(0, col.shape[0], 128):
        own = lanes((128, 128)) == lax.broadcasted_iota(jnp.int32, (128, 128), 0)
        pieces.append(jnp.sum(jnp.where(own, col[start : start + 128], 0), 0, keepdims=True))
    return jnp.concatenate(pieces, 1)


def whole(shape):
    return pl.BlockSpec(shape, lambda *_: (0,) * len(shape))


def params(limit):
    return pltpu.CompilerParams(vmem_limit_bytes=limit * MIB)


def cost(macs, moved, exps=0):
    return pl.CostEstimate(flops=2 * macs, bytes_accessed=moved, transcendentals=exps)


def teacher_mix_kernel(x_ref, gain_ref, wq_ref, wk_ref, wv_ref, bq_ref, bk_ref, bv_ref, out_ref, normed):
    @pl.when(pl.program_id(0) == 0)
    def _():
        normed[...] = layer_norm(x_ref[...].astype(F32), gain_ref[...]).astype(BF16)

    rows = normed[...]
    for part, (w_ref, b_ref) in enumerate(((wq_ref, bq_ref), (wk_ref, bk_ref), (wv_ref, bv_ref))):
        mixed = (dot(rows, w_ref[...]) + b_ref[...]).astype(BF16).astype(F32)
        if part == 0:
            mixed = mixed * HD_V ** (-0.5)
        turned = mixed.T.astype(BF16)
        for head in range(turned.shape[0] // HD_V):
            piece = turned[head * HD_V : (head + 1) * HD_V]
            for core in range(2):
                out_ref[2 * head + core, part * HD_V : (part + 1) * HD_V, :] = piece


def teacher_mix(patches, gain, weights, bias):
    rows, width = patches.shape
    heads = width // HD_V
    step = 256
    steps = width // step

    def col(part):
        return pl.BlockSpec((width, step), lambda i: (0, part * steps + i))

    def bias_col(part):
        return pl.BlockSpec((1, step), lambda i: (0, part * steps + i))

    return pl.pallas_call(
        teacher_mix_kernel,
        grid=(steps,),
        in_specs=[whole((rows, width)), whole((1, width))]
        + [col(p) for p in range(3)]
        + [bias_col(p) for p in range(3)],
        out_specs=pl.BlockSpec((2 * step // HD_V, 3 * HD_V, rows), lambda i: (i, 0, 0)),
        out_shape=jax.ShapeDtypeStruct((2 * heads, 3 * HD_V, rows), BF16),
        scratch_shapes=[pltpu.VMEM((rows, width), BF16)],
        compiler_params=params(60),
        cost_estimate=cost(rows * width * 3 * width, 8 * MIB),
        name="teacher_mix",
    )(patches, gain, weights, weights, weights, bias, bias, bias)


BOUND = 60.0
TILES = 4


def teacher_attention_kernel(core_ref, mix_ref, out_ref, safe, keys, values, scores):
    tiles, _, rows = mix_ref.shape
    step = pl.program_id(0)
    core = core_ref[0]
    count = tiles * rows

    @pl.when(step == 0)
    def _():
        peaks = [None, None]
        for tile in range(tiles):
            span = slice(tile * rows, (tile + 1) * rows)
            keys[:, span] = mix_ref[tile, HD_V : 2 * HD_V, :]
            turned = mix_ref[tile, 2 * HD_V :, :].astype(F32)
            values[span, :] = jnp.concatenate([turned, jnp.ones_like(turned)], 0).T.astype(BF16)
            for part in range(2):
                piece = mix_ref[tile, part * HD_V : (part + 1) * HD_V, :].astype(F32)
                norms = jnp.sum(piece * piece, 0, keepdims=True)
                peaks[part] = norms if peaks[part] is None else jnp.maximum(peaks[part], norms)
        bound = jnp.max(peaks[0], -1, keepdims=True) * jnp.max(peaks[1], -1, keepdims=True)
        safe[0] = (jnp.max(bound) <= BOUND * BOUND).astype(jnp.int32)

    first = TILES * step
    queries = [mix_ref[2 * (first + i) + core, :HD_V, :].astype(F32) for i in range(TILES)]
    queries = jnp.concatenate(queries, 1).T.astype(BF16)

    def finish(total):
        turned = total.T
        attended = (turned[:HD_V] / turned[HD_V:]).astype(BF16)
        for i in range(TILES):
            out_ref[i] = attended[:, i * rows : (i + 1) * rows]

    @pl.when(safe[0] == 1)
    def _():
        chunk = 512
        total, waiting = None, None
        for start in list(range(0, count, chunk)) + [None]:
            part = None if start is None else dot(queries, keys[:, start : start + chunk])
            if waiting is not None:
                added = dot(waiting[1], values[waiting[0] : waiting[0] + chunk, :])
                total = added if total is None else total + added
            if start is not None:
                waiting = (start, jnp.exp(part).astype(BF16))
        finish(total)

    @pl.when(safe[0] == 0)
    def _():
        chunk = 1024
        top = None
        for start in range(0, count, chunk):
            part = dot(queries, keys[:, start : start + chunk])
            scores[:, start : start + chunk] = part
            peak = jnp.max(part, -1, keepdims=True)
            top = peak if top is None else jnp.maximum(top, peak)
        total = None
        for start in range(0, count, chunk):
            exps = jnp.exp(scores[:, start : start + chunk] - top).astype(BF16)
            part = dot(exps, values[start : start + chunk, :])
            total = part if total is None else total + part
        finish(total)


def teacher_attention(core, mix):
    tiles, depth, rows = mix.shape
    return pl.pallas_call(
        teacher_attention_kernel,
        grid_spec=pltpu.PrefetchScalarGridSpec(
            num_scalar_prefetch=1,
            grid=(tiles // 2 // TILES,),
            in_specs=[whole((tiles, depth, rows))],
            out_specs=pl.BlockSpec((TILES, HD_V, rows), lambda i, c: (i, 0, 0)),
            scratch_shapes=[
                pltpu.SMEM((1,), jnp.int32),
                pltpu.VMEM((HD_V, tiles * rows), BF16),
                pltpu.VMEM((tiles * rows, 128), BF16),
                pltpu.VMEM((TILES * rows, tiles * rows), F32),
            ],
        ),
        out_shape=jax.ShapeDtypeStruct((tiles // 2, HD_V, rows), BF16),
        compiler_params=params(28),
        cost_estimate=cost(2 * tiles * rows * tiles * rows * 128, 2 * MIB, tiles * rows * tiles * rows // 2),
        name="teacher_attention",
    )(core, mix)


def teacher_reply_kernel(me_ref, att_ref, patches_ref, proj_ref, scale_ref, head_ref, asked_ref, out_ref, seen):
    @pl.when(pl.program_id(0) == 0)
    def _():
        heads, depth, rows = att_ref.shape
        attended = att_ref[...].reshape(heads * depth, rows).astype(F32).T.astype(BF16)
        teacher = (patches_ref[...].astype(F32) + scale_ref[...] * dot(attended, proj_ref[...])).astype(BF16)
        through = dot(teacher, head_ref[...], NT)
        wide = teacher.astype(F32)
        seen[...] = (through * lax.rsqrt(jnp.sum(wide * wide, -1, keepdims=True) + eps_norm)).astype(BF16)

    asked = asked_ref[...]
    mine = jnp.sum(jnp.where(lanes(asked.shape) == me_ref[0], asked, 0), -1, keepdims=True)
    hot = jnp.where(lanes((asked.shape[0], seen.shape[0])) == mine - 1, 1.0, 0.0).astype(BF16)
    out_ref[...] = dot(hot, seen[...]).astype(BF16)


def teacher_reply(me, attended, patches, proj, scale, head, asked):
    rows, width = patches.shape
    points = head.shape[0]
    total, devices = asked.shape
    step = total // 6
    return pl.pallas_call(
        teacher_reply_kernel,
        grid_spec=pltpu.PrefetchScalarGridSpec(
            num_scalar_prefetch=1,
            grid=(total // step,),
            in_specs=[
                whole(attended.shape),
                whole((rows, width)),
                whole(proj.shape),
                whole((1, width)),
                whole(head.shape),
                pl.BlockSpec((step, devices), lambda i, m: (i, 0)),
            ],
            out_specs=pl.BlockSpec((step, points), lambda i, m: (i, 0)),
            scratch_shapes=[pltpu.VMEM((rows, points), BF16)],
        ),
        out_shape=jax.ShapeDtypeStruct((total, points), BF16),
        compiler_params=params(60),
        cost_estimate=cost(rows * width * (width + points) + total * rows * points, 9 * MIB),
        name="teacher_reply",
    )(me, attended, patches, proj, scale, head, asked)


def request_kernel(tile_ref, patch_ref, place_ref, asked_ref):
    count = tile_ref.shape[1]
    width = asked_ref.shape[1]
    block = 256
    earlier_than = jnp.where(
        lax.broadcasted_iota(jnp.int32, (block, block), 0) < lanes((block, block)), 1.0, 0.0
    ).astype(BF16)
    before = jnp.zeros((width, 1), F32)
    asked = jnp.zeros((32, width), F32)
    for start in range(0, count, block):
        span = slice(start, start + block)
        tiles = tile_ref[:, span]
        hot = jnp.where(lax.broadcasted_iota(jnp.int32, (width, block), 0) == tiles, 1.0, 0.0)
        earlier = dot(hot.astype(BF16), earlier_than) + before
        before = before + jnp.sum(hot, 1, keepdims=True)
        slot = jnp.sum(earlier * hot, 0, keepdims=True).astype(jnp.int32)
        place_ref[:, span] = tiles * CAP + slot
        slot_hot = jnp.where(lax.broadcasted_iota(jnp.int32, (32, block), 0) == slot, 1.0, 0.0)
        named = (hot * (patch_ref[:, span] + 1).astype(F32)).astype(BF16)
        asked = asked + dot(slot_hot.astype(BF16), named, NT)
    asked_ref[...] = asked[:CAP].astype(jnp.int32)


def requests(tile_ids, patch_ids, devices):
    count = tile_ids.shape[1]
    return pl.pallas_call(
        request_kernel,
        out_shape=(
            jax.ShapeDtypeStruct((1, count), jnp.int32),
            jax.ShapeDtypeStruct((CAP, devices), jnp.int32),
        ),
        compiler_params=params(60),
        cost_estimate=cost(count * 128 * 512, MIB),
        name="requests",
    )(tile_ids, patch_ids)


def point_mix_kernel(order_ref, feats_ref, gain_ref, w_ref, serial_ref, query_ref, pair_ref, peak_ref):
    rows, count = order_ref.shape[1], feats_ref.shape[0]
    hot = jnp.where(lanes((rows, count)) == column(order_ref[...]), 1.0, 0.0).astype(BF16)
    serial = dot(hot, feats_ref[...])
    serial_ref[...] = serial.astype(BF16)
    normed = layer_norm(serial, gain_ref[...]).astype(BF16)
    mixed = dot(normed, w_ref[...]).astype(BF16).astype(F32)
    width = w_ref.shape[1]
    scale = jnp.where(lanes((1, width)) < width // 3, HD_P ** (-0.5), 1.0)
    mixed = mixed * scale
    att = width // 3
    query_ref[...] = mixed[:, :att].astype(BF16)
    for piece in range(2 * att // 128):
        pair_ref[piece] = mixed[:, att + piece * 128 : att + (piece + 1) * 128].astype(BF16)
    head = lax.broadcasted_iota(jnp.int32, (att, att), 0) // HD_P
    head_sum = jnp.where(head == lanes((att, att)) // HD_P, 1.0, 0.0).astype(BF16)
    for part in range(2):
        piece = mixed[:, part * att : (part + 1) * att]
        norms = dot((piece * piece).astype(BF16), head_sum)
        peak = jnp.max(norms, 0, keepdims=True)
        peak_ref[:, part * att : (part + 1) * att] = jnp.broadcast_to(peak, (8, att))


def point_mix(order, feats, gain, weights):
    count, width = feats.shape
    step = MIX_STEP
    att = weights.shape[1] // 3
    return pl.pallas_call(
        point_mix_kernel,
        grid=(count // step,),
        in_specs=[
            pl.BlockSpec((1, step), lambda i: (0, i)),
            whole((count, width)),
            whole((1, width)),
            whole(weights.shape),
        ],
        out_specs=(
            pl.BlockSpec((step, width), lambda i: (i, 0)),
            pl.BlockSpec((step, att), lambda i: (i, 0)),
            pl.BlockSpec((2 * att // 128, step, 128), lambda i: (0, i, 0)),
            pl.BlockSpec((8, 2 * att), lambda i: (i, 0)),
        ),
        out_shape=(
            jax.ShapeDtypeStruct((count, width), BF16),
            jax.ShapeDtypeStruct((count, att), BF16),
            jax.ShapeDtypeStruct((2 * att // 128, count, 128), BF16),
            jax.ShapeDtypeStruct((8 * count // step, 2 * att), F32),
        ),
        compiler_params=params(28),
        cost_estimate=cost(count * width * (count + weights.shape[1]), 9 * MIB),
        name="point_mix",
    )(order, feats, gain, weights)


ROWS = 128
KEYS = 256
GROUP = 128 // HD_P
PARTS = 2


def window_attention_kernel(
    first,
    base_ref,
    count_ref,
    query_ref,
    pair_ref,
    peak_ref,
    window_ref,
    out_ref,
    safe,
    pairs,
    query_mark,
    key_mark,
    stack,
    top,
    total,
):
    points, att = pair_ref.shape[1], query_ref.shape[1]
    groups = att // 128
    stacked = GROUP * ROWS

    @pl.when(pl.program_id(0) == 0)
    def _():
        pairs[...] = pair_ref[...].astype(F32)
        slot = lax.broadcasted_iota(jnp.int32, (128, 128), 0)
        for start in range(0, points, 128):
            window = window_ref[:, start : start + 128]
            other = jnp.where((slot < 4) & (slot != window), -BIG, 0.0)
            key_mark[start : start + 128, :] = other.T
            query_mark[start : start + 128, :] = jnp.where(slot == window, 1.0, 0.0).T.astype(BF16)
        peak = jnp.max(peak_ref[...], 0, keepdims=True)
        safe[0] = (jnp.max(peak[:, :att] * peak[:, att:]) <= BOUND * BOUND).astype(jnp.int32)

    block = pl.program_id(0) + first
    base = base_ref[block]
    steps = count_ref[block]
    here = pl.ds(pl.multiple_of(block * ROWS, ROWS), ROWS)
    lane_head = lanes((ROWS, 128)) // HD_P
    for group in range(groups):
        queries = query_ref[:, group * 128 : (group + 1) * 128]
        for head in range(GROUP):
            span = slice(group * stacked + head * ROWS, group * stacked + (head + 1) * ROWS)
            stack[span, :128] = jnp.where(lane_head == head, queries, jnp.zeros_like(queries))
            stack[span, 128:] = query_mark[here, :]
    def span_of(step, size):
        return pl.ds(base + step * KEYS, size)

    def keys_of(group, span):
        return jnp.concatenate([pairs[group, span, :], key_mark[span, :]], 1).astype(BF16)

    def values_of(group, span):
        values = pairs[groups + group, span, :].astype(BF16)
        return jnp.concatenate([values, jnp.ones_like(values)], 1)

    def fold(step, size):
        span = span_of(step, size)
        rows = stacked // PARTS * 2
        waiting = None

        def add(span, exps, values):
            total[span, :] = jnp.where(step == 0, 0.0, total[span, :]) + dot(exps, values)

        for group in range(groups):
            keys, values = keys_of(group, span), values_of(group, span)
            for start in range(group * stacked, (group + 1) * stacked, rows):
                part = dot(stack[start : start + rows, :], keys, NT)
                if waiting is not None:
                    add(*waiting)
                waiting = (slice(start, start + rows), jnp.exp(part).astype(BF16), values)
        add(*waiting)

    @pl.when(safe[0] == 1)
    def _():
        @pl.loop(0, steps // 4)
        def _(step):
            fold(4 * step, 4 * KEYS)

        @pl.when(steps % 4 >= 2)
        def _():
            fold(steps // 4 * 4, 2 * KEYS)

        @pl.when(steps % 2 == 1)
        def _():
            fold(steps - 1, KEYS)

    @pl.when(safe[0] == 0)
    def _():
        total[...] = jnp.zeros(total.shape, F32)
        for group in range(groups):
            rows = slice(group * stacked, (group + 1) * stacked)
            top[...] = jnp.full(top.shape, -BIG, F32)

            @pl.loop(0, steps)
            def _(step):
                part = dot(stack[rows, :], keys_of(group, span_of(step, KEYS)), NT)
                top[...] = jnp.maximum(top[...], jnp.maximum(part[:, :128], part[:, 128:]))

            top[...] = jnp.broadcast_to(jnp.max(top[...], -1, keepdims=True), top.shape)

            @pl.loop(0, steps)
            def _(step):
                span = span_of(step, KEYS)
                part = dot(stack[rows, :], keys_of(group, span), NT)
                peak = top[...]
                exps = jnp.exp(part - jnp.concatenate([peak, peak], 1)).astype(BF16)
                total[rows, :] += dot(exps, values_of(group, span))

    for group in range(groups):
        over, under = None, None
        for head in range(GROUP):
            span = slice(group * stacked + head * ROWS, group * stacked + (head + 1) * ROWS)
            own = lane_head == head
            over = total[span, :128] if over is None else jnp.where(own, total[span, :128], over)
            under = total[span, 128:] if under is None else jnp.where(own, total[span, 128:], under)
        out_ref[:, group * 128 : (group + 1) * 128] = (over / under).astype(BF16)


def window_ranges(windows):
    points = windows.shape[0]
    blocks = windows.reshape(points // ROWS, ROWS)
    start = jnp.sum((windows[None, :] < blocks[:, :1]).astype(jnp.int32), 1)
    end = jnp.sum((windows[None, :] <= blocks[:, -1:]).astype(jnp.int32), 1)
    count = (end - start + KEYS - 1) // KEYS
    base = jnp.minimum(start, points - count * KEYS)
    return base, count


def window_attention(queries, pairs, peaks, window_row, base, count, first, blocks):
    points, att = queries.shape
    stacked = GROUP * ROWS
    return pl.pallas_call(
        functools.partial(window_attention_kernel, first),
        grid_spec=pltpu.PrefetchScalarGridSpec(
            num_scalar_prefetch=2,
            grid=(blocks,),
            in_specs=[pl.BlockSpec((ROWS, att), lambda i, b, c: (i + first, 0)), whole(pairs.shape), whole(peaks.shape), whole((1, points))],
            out_specs=pl.BlockSpec((ROWS, att), lambda i, b, c: (i, 0)),
            scratch_shapes=[
                pltpu.SMEM((1,), jnp.int32),
                pltpu.VMEM(pairs.shape, F32),
                pltpu.VMEM((points, 128), BF16),
                pltpu.VMEM((points, 128), F32),
                pltpu.VMEM((att // 128 * stacked, 256), BF16),
                pltpu.VMEM((stacked, 128), F32),
                pltpu.VMEM((att // 128 * stacked, 256), F32),
            ],
        ),
        out_shape=jax.ShapeDtypeStruct((blocks * ROWS, att), BF16),
        compiler_params=params(40),
        cost_estimate=cost(
            blocks * ROWS * 1024 * 16 * 512, 5 * MIB, blocks * ROWS * 1024 * 16
        ),
        name="window_attention",
    )(base, count, queries, pairs, peaks, window_row)


def point_block_kernel(serial_ref, att_ref, proj_ref, gain_ref, up_ref, down_ref, head_ref, out_ref, norm_ref):
    residual = serial_ref[...].astype(F32) + dot(att_ref[...], proj_ref[...])
    normed = layer_norm(residual, gain_ref[...]).astype(BF16)
    hidden_width = up_ref.shape[1]
    chunk = HIDDEN
    added = None
    for start in range(0, hidden_width, chunk):
        before = dot(normed, up_ref[:, start : start + chunk])
        hidden = (0.5 * before * (1.0 + lax.erf(before * (0.5**0.5)))).astype(BF16)
        part = dot(hidden, down_ref[start : start + chunk, :])
        added = part if added is None else added + part
    block_out = (residual + added).astype(BF16)
    out_ref[...] = block_out
    student = dot(block_out, head_ref[...])
    norm_ref[...] = row_of(jnp.sum(student * student, -1, keepdims=True))


def point_block(serial, attended, proj, gain, up, down, head):
    count, width = serial.shape
    att = attended.shape[1]
    step = BLOCK_STEP
    return pl.pallas_call(
        point_block_kernel,
        grid=(count // step,),
        in_specs=[
            pl.BlockSpec((step, width), lambda i: (i, 0)),
            pl.BlockSpec((step, att), lambda i: (i, 0)),
            whole(proj.shape),
            whole((1, width)),
            whole(up.shape),
            whole(down.shape),
            whole(head.shape),
        ],
        out_specs=(
            pl.BlockSpec((step, width), lambda i: (i, 0)),
            pl.BlockSpec((1, step), lambda i: (0, i)),
        ),
        out_shape=(
            jax.ShapeDtypeStruct((count, width), BF16),
            jax.ShapeDtypeStruct((1, count), F32),
        ),
        compiler_params=params(36),
        cost_estimate=cost(
            count * width * (att + 2 * up.shape[1] + head.shape[1]), 12 * MIB, count * up.shape[1]
        ),
        name="point_block",
    )(serial, attended, proj, gain, up, down, head)


def loss_kernel(place_ref, out_ref, norm_ref, replies_ref, loss_ref):
    rows, total = place_ref.shape[1], replies_ref.shape[0]
    hot = jnp.where(lanes((rows, total)) == column(place_ref[...]), 1.0, 0.0).astype(BF16)
    target = dot(hot, replies_ref[...])
    inner = jnp.sum(out_ref[...].astype(F32) * target, -1, keepdims=True)
    loss_ref[...] = 1.0 - row_of(inner) * lax.rsqrt(norm_ref[...] + eps_norm)


def loss(place, point_out, norms, replies):
    count, width = point_out.shape
    step = LOSS_STEP
    return pl.pallas_call(
        loss_kernel,
        grid=(count // step,),
        in_specs=[
            pl.BlockSpec((1, step), lambda i: (0, i)),
            pl.BlockSpec((step, width), lambda i: (i, 0)),
            pl.BlockSpec((1, step), lambda i: (0, i)),
            whole(replies.shape),
        ],
        out_specs=pl.BlockSpec((1, step), lambda i: (0, i)),
        out_shape=jax.ShapeDtypeStruct((1, count), F32),
        compiler_params=params(60),
        cost_estimate=cost(count * width * replies.shape[0], 8 * MIB),
        name="loss",
    )(place, point_out, norms, replies)


def local(
    patches,
    vit_gain,
    vit_qkv,
    vit_qkv_bias,
    vit_proj,
    vit_scale,
    point_feats,
    point_order,
    window_ids,
    point_tile,
    point_patch,
    pt_gain,
    pt_qkv,
    pt_proj,
    pt_up,
    pt_down,
    head_w,
):
    both = ("cam", "tile")
    tile_count = lax.axis_size("tile")
    device_count = lax.axis_size("cam") * tile_count
    tile_index = lax.axis_index("tile")
    me = (lax.axis_index("cam") * tile_count + tile_index).astype(jnp.int32).reshape(1)
    core = (tile_index % 2).astype(jnp.int32).reshape(1)
    count = point_feats.shape[0]

    mix = teacher_mix(patches[0], vit_gain[None], vit_qkv, vit_qkv_bias[None])
    mix = lax.all_to_all(mix, "tile", split_axis=0, concat_axis=0, tiled=True)

    place, asked = requests(point_tile.reshape(1, count), point_patch.reshape(1, count), device_count)
    asked = lax.all_gather(asked, both, axis=0, tiled=True)
    serial, queries, pairs, peaks = point_mix(
        point_order, point_feats, pt_gain[:1], pt_qkv
    )
    base, steps = window_ranges(window_ids[0])
    blocks = count // ROWS
    cuts = (0, blocks // 8, 7 * blocks // 16, blocks)

    def attend(part, base):
        return window_attention(
            queries, pairs, peaks, window_ids, base, steps, cuts[part], cuts[part + 1] - cuts[part]
        )

    parts = [attend(0, base)]
    mix, parts[0] = lax.optimization_barrier((mix, parts[0]))
    attended = teacher_attention(core, mix)
    groups = [[2 * i + c for i in range(tile_count // 2)] for c in range(2)]
    attended, base = lax.optimization_barrier((attended, base))
    attended = lax.all_to_all(
        attended, "tile", split_axis=0, concat_axis=0, tiled=True, axis_index_groups=groups
    )
    parts.append(attend(1, base))
    attended, parts[1], base = lax.optimization_barrier((attended, parts[1], base))
    replies = teacher_reply(me, attended, patches[0], vit_proj, vit_scale[None], head_w, asked)
    replies, base = lax.optimization_barrier((replies, base))
    replies = lax.all_to_all(
        replies.reshape(device_count, CAP, -1), both, split_axis=0, concat_axis=0, tiled=True
    ).reshape(device_count * CAP, -1)
    parts.append(attend(2, base))
    pt_attended = jnp.concatenate(parts, 0)
    point_out, norms = point_block(serial, pt_attended, pt_proj, pt_gain[1:], pt_up, pt_down, head_w)
    losses = loss(place, point_out, norms, replies)
    return (point_out, losses.reshape(count))


def solution(mesh):
    both = ("cam", "tile")
    placed = (
        P("cam", "tile", None),
        P(),
        P(),
        P(),
        P(),
        P(),
        P(both, None),
        P(both, None),
        P(both, None),
        P(both, None),
        P(both),
        P(),
        P(),
        P(),
        P(),
        P(),
        P(),
    )
    return jax.shard_map(
        local,
        mesh=mesh,
        in_specs=placed,
        out_specs=(P(both, None), P(both)),
        check_vma=False,
    )
```
